256 devices in a mesh: dp: 64 (over y_hi, z, x), tensor: 4 (over y_lo, core).
Axes of the slice: x: 4, y: 4 (y_hi: 2, y_lo: 2; y = y_hi * 2 + y_lo), z: 8, core: 2. Of those that a mesh axis runs over, the one named last changes fastest.
Arguments:
- image_vectors_raw: bfloat16 [16384, 1152], P('dp'), may hold values from -0.5 to 0.5
- text_vectors_raw: bfloat16 [16384, 1152], P('dp'), may hold values from -0.5 to 0.5
- logit_scale_logarithm: float32 [1], replicated, may hold values from 2 to 3
- logit_offset_bias: float32 [1], replicated, may hold values from -10 to -7
Outputs:
- grad_image: float32 [16384, 1152], P(('dp', 'tensor'))
- grad_text: float32 [16384, 1152], P(('dp', 'tensor'))
- image_loss: float32 [16384], P(('dp', 'tensor'))
- text_loss: float32 [16384], P(('dp', 'tensor'))
- param_grads: float32 [2], replicated
The draws below stay inside these ranges and needn't reach their ends.
All inputs are finite; a program needn't handle non-finite values.
Results may differ from the reference program's by a relative error of at most 0.0023.
Values may be sent and summed in bfloat16 or wider, within the bound.
No kernel may reach another device: no remote copies, remote signals or barrier semaphores. Data moves between devices by JAX's collectives and lax.ppermute only.
A program may use at most 64 MiB of HBM per device.

```python
import math
import jax
import jax.numpy as jnp
from jax import lax

D = 1152
TOK = 256
BATCH = 16384
N_DP = 64


def law_values(base_key, array_shape):
    bell_values = jax.random.truncated_normal(jax.random.fold_in(base_key, 1), -3.0, 3.0, array_shape, jnp.float32)
    return bell_values


def shared_parts(base_key, ramp_top, strength_low, strength_high):
    groups = max(2, BATCH // 32)
    feature_scale = jnp.exp(jax.random.uniform(jax.random.fold_in(base_key, 101), (D,), jnp.float32) * math.log(10.0))
    centers = law_values(jax.random.fold_in(base_key, 102), (groups, D))
    members = jax.random.randint(jax.random.fold_in(base_key, 103), (BATCH,), 0, groups)
    private = law_values(jax.random.fold_in(base_key, 104), (BATCH, D))
    common = law_values(jax.random.fold_in(base_key, 105), (1, D))
    position = jnp.arange(BATCH, dtype=jnp.float32) / float(max(BATCH - 1, 1))
    spread = jax.random.uniform(jax.random.fold_in(base_key, 106), (BATCH,), jnp.float32)
    strength = strength_low * jnp.exp(spread * math.log(strength_high / strength_low) + position * math.log(ramp_top))
    return (feature_scale, centers[members], private, common, strength)


def embed_rows(shared, own_key, scale_top, common_weight):
    feature_scale, center_rows, private, common, strength = shared
    row_count = center_rows.shape[0]
    own_noise = law_values(jax.random.fold_in(own_key, 201), center_rows.shape)
    jitter = jnp.exp(jax.random.uniform(jax.random.fold_in(own_key, 202), (row_count, 1), jnp.float32, -0.2, 0.2))
    row_scale = jnp.exp(jax.random.uniform(jax.random.fold_in(own_key, 203), (row_count, 1), jnp.float32) * math.log(scale_top))
    mixture = strength[:, None] * jitter * center_rows + private + 0.5 * own_noise + common_weight * common
    values = 0.001 * row_scale * feature_scale[None, :] * mixture
    return jnp.clip(values, -0.5, 0.5).astype(jnp.bfloat16)


def draw_image_vectors_raw(key, part):
    scale_top, common_weight = (10.0, 0.1)
    shared = shared_parts(key, 3.0, 0.3, 1.0)
    key = jax.random.fold_in(key, 7)
    return embed_rows(shared, key, scale_top, common_weight)


def draw_text_vectors_raw(key, part):
    scale_top, common_weight = (10.0, 0.1)
    shared = shared_parts(key, 3.0, 0.3, 1.0)
    key = jax.random.fold_in(key, 13)
    return embed_rows(shared, key, scale_top, common_weight)


def setup_inputs(seed: int = 0) -> dict:
    seeds = jax.random.split(jax.random.key(seed), 5)
    image_vectors_raw = draw_image_vectors_raw(jax.random.fold_in(seeds[4], 71), 0)
    text_vectors_raw = draw_text_vectors_raw(jax.random.fold_in(seeds[4], 71), 0)
    logit_scale_logarithm = jnp.clip(jax.random.uniform(seeds[2], (1,), jnp.float32, 2.0, 3.0), 2.0, 3.0)
    logit_offset_bias = jnp.clip(jax.random.uniform(seeds[3], (1,), jnp.float32, -10.0, -7.0), -10.0, -7.0)
    return dict(image_vectors_raw=image_vectors_raw, text_vectors_raw=text_vectors_raw, logit_scale_logarithm=logit_scale_logarithm, logit_offset_bias=logit_offset_bias)


def normalize(embedding):
    floats = embedding.astype(jnp.float32)
    inverse = lax.rsqrt(lax.optimization_barrier(jnp.sum(floats * floats, axis=-1, keepdims=True)) + 1e-06)
    return (floats * inverse, inverse)

def reference(image_vectors_raw, text_vectors_raw, logit_scale_logarithm, logit_offset_bias):
    image_unit, image_inv = normalize(image_vectors_raw)
    text_unit, text_inv = normalize(text_vectors_raw)
    image_reduced_precision = image_unit.astype(jnp.bfloat16)
    text_reduced_precision = text_unit.astype(jnp.bfloat16)
    logit_scale_factor = jnp.exp(logit_scale_logarithm[0])
    block_shift_amount = logit_offset_bias[0]
    total_rows = image_vectors_raw.shape[0]
    columns = jnp.arange(total_rows, dtype=jnp.int32)

    def stepper(carry_state, block_index):
        back_grad, back_loss, sum_bias, scale_gradient_sum = carry_state
        start_row = (block_index * TOK).astype(jnp.int32)
        left_block_rows = lax.dynamic_slice_in_dim(image_reduced_precision, start_row, TOK, 0)
        row_ids = start_row + jnp.arange(TOK, dtype=jnp.int32)
        positive = (row_ids[:, None] == columns[None, :]).astype(jnp.float32)
        similarity_scores = jnp.dot(left_block_rows, text_reduced_precision.T, preferred_element_type=jnp.float32)
        pair_logit_matrix = logit_scale_factor * similarity_scores + block_shift_amount
        losses = jax.nn.softplus(pair_logit_matrix) - positive * pair_logit_matrix
        sigmoid_derivatives = jax.nn.sigmoid(pair_logit_matrix) - positive
        pair_weight_factors = (logit_scale_factor * sigmoid_derivatives).astype(jnp.bfloat16)
        front_rows = jnp.dot(pair_weight_factors, text_reduced_precision, preferred_element_type=jnp.float32)
        back_grad = back_grad + jnp.dot(pair_weight_factors.T, left_block_rows, preferred_element_type=jnp.float32)
        back_loss = back_loss + lax.optimization_barrier(jnp.sum(losses, axis=0))
        sum_bias = sum_bias + jnp.sum(sigmoid_derivatives)
        scale_gradient_sum = scale_gradient_sum + logit_scale_factor * jnp.sum(sigmoid_derivatives * similarity_scores)
        return ((back_grad, back_loss, sum_bias, scale_gradient_sum), (front_rows, lax.optimization_barrier(jnp.sum(losses, axis=1))))
    initial = (jnp.zeros((total_rows, D), jnp.float32), jnp.zeros((total_rows,), jnp.float32), jnp.zeros((), jnp.float32), jnp.zeros((), jnp.float32))
    carry_state, outputs = lax.scan(stepper, initial, jnp.arange(N_DP, dtype=jnp.int32))
    back_grad, text_loss, sum_bias, scale_gradient_sum = carry_state
    front_grad = outputs[0].reshape(total_rows, D)
    image_loss = outputs[1].reshape(total_rows)
    grad_image = image_inv * (front_grad - image_unit * lax.optimization_barrier(jnp.sum(image_unit * front_grad, axis=-1, keepdims=True)))
    grad_text = text_inv * (back_grad - text_unit * lax.optimization_barrier(jnp.sum(text_unit * back_grad, axis=-1, keepdims=True)))
    param_grads = jnp.stack([scale_gradient_sum, sum_bias])
    return (grad_image, grad_text, image_loss, text_loss, param_grads)
```

```python
import jax
import jax.numpy as jnp
from jax import lax
from jax.experimental import pallas as pl
from jax.experimental.pallas import tpu as pltpu
from jax.sharding import Mesh, PartitionSpec as P

AXES = ("yh", "z", "x", "yl", "core")
YH, NZ, NX, YL, NC = 2, 8, 4, 2, 2
Q = 64


def table(move):
    pairs = []
    for yh in range(YH):
        for z in range(NZ):
            for x in range(NX):
                for yl in range(YL):
                    for c in range(NC):
                        y2, z2, x2, c2 = move(yh * 2 + yl, z, x, c)
                        y2, z2, x2 = y2 % 4, z2 % NZ, x2 % NX
                        source = (((yh * NZ + z) * NX + x) * YL + yl) * NC + c
                        target = (((y2 // 2 * NZ + z2) * NX + x2) * YL + y2 % 2) * NC + c2
                        pairs.append((source, target))
    return pairs


def send(value, dx=0, dz=0, fy=0, fz=0, fx=0, fc=0):
    pairs = table(lambda y, z, x, c: (y ^ fy, (z + dz) ^ fz, (x + dx) ^ fx, c ^ fc))
    return lax.ppermute(value, AXES, pairs)


def normalize(embedding):
    floats = embedding.astype(jnp.float32)
    inverse = lax.rsqrt(jnp.sum(floats * floats, axis=-1, keepdims=True) + 1e-06)
    return (floats * inverse, inverse)


ROWS = 256


def pair_kernel(par_ref, *refs):
    img_in = refs[:16]
    txt_in = refs[16:24]
    gi_ref, gt_ref, li_ref, lt_ref, sums_ref, img, txt = refs[24:]
    for k in range(16):
        img[k * Q : (k + 1) * Q, :] = img_in[k][...]
    for k in range(8):
        txt[k * 2 * Q : (k + 1) * 2 * Q, :] = txt_in[k][...]
    temperature = par_ref[0]
    offset = par_ref[1]
    texts = txt[...]
    loss_cols = None
    slope_sum = None
    scale_sum = None
    for r in range(1024 // ROWS):
        images = img[r * ROWS : (r + 1) * ROWS, :]
        scores = lax.dot_general(
            images, texts, (((1,), (1,)), ((), ())), preferred_element_type=jnp.float32
        )
        logits = scores * temperature + offset
        p = jnp.exp(logits)
        q = 1.0 + p
        slopes = p / q
        losses = jnp.where(p < 0.0009765625, p - 0.5 * p * p, jnp.log(q))
        if r == 0:
            eye = (
                lax.broadcasted_iota(jnp.int32, (ROWS, 1024), 0)
                == lax.broadcasted_iota(jnp.int32, (ROWS, 1024), 1)
            ) & (lax.broadcasted_iota(jnp.int32, (ROWS, 1024), 0) < Q)
            slopes = jnp.where(eye, slopes - 1.0, slopes)
            losses = jnp.where(eye, losses - logits, losses)
        weights = (temperature * slopes).astype(jnp.bfloat16)
        gi_ref[r * ROWS : (r + 1) * ROWS, :] = jnp.dot(
            weights, texts, preferred_element_type=jnp.float32
        )
        back = lax.dot_general(
            weights, images, (((0,), (0,)), ((), ())), preferred_element_type=jnp.float32
        )
        li_ref[r * ROWS : (r + 1) * ROWS, :] = jnp.sum(losses, axis=1, keepdims=True)
        cols = jnp.sum(losses, axis=0, keepdims=True)
        s1 = jnp.sum(slopes, axis=0, keepdims=True)
        s2 = jnp.sum(slopes * scores, axis=0, keepdims=True)
        if r == 0:
            gt_ref[...] = back
            loss_cols, slope_sum, scale_sum = cols, s1, s2
        else:
            gt_ref[...] += back
            loss_cols, slope_sum, scale_sum = loss_cols + cols, slope_sum + s1, scale_sum + s2
    lt_ref[...] = loss_cols
    sums_ref[0:1, :] = slope_sum
    sums_ref[1:2, :] = temperature * scale_sum


def pairs_on_device(params, image_chunks, text_chunks):
    width = image_chunks[0].shape[1]
    vmem = pl.BlockSpec(memory_space=pltpu.VMEM)
    f32 = jnp.float32
    return pl.pallas_call(
        pair_kernel,
        out_shape=(
            jax.ShapeDtypeStruct((1024, width), f32),
            jax.ShapeDtypeStruct((1024, width), f32),
            jax.ShapeDtypeStruct((1024, 1), f32),
            jax.ShapeDtypeStruct((1, 1024), f32),
            jax.ShapeDtypeStruct((2, 1024), f32),
        ),
        in_specs=[pl.BlockSpec(memory_space=pltpu.SMEM)] + [vmem] * 24,
        out_specs=(vmem,) * 5,
        scratch_shapes=[
            pltpu.VMEM((1024, width), jnp.bfloat16),
            pltpu.VMEM((1024, width), jnp.bfloat16),
        ],
        compiler_params=pltpu.CompilerParams(vmem_limit_bytes=48 * 1024 * 1024),
        cost_estimate=pl.CostEstimate(
            flops=6 * 1024 * 1024 * width, bytes_accessed=14 * 1024 * 1024, transcendentals=3 * 1024 * 1024
        ),
        name="pairs",
    )(params, *image_chunks, *text_chunks)


def gather_images(own, partner):
    got = {0: own}
    up = down = own
    for step in range(1, 4):
        up, down = send(up, dz=1), send(down, dz=-1)
        got[-step % 8], got[step] = up, down
    got[4] = send(up, dz=1)
    mine = [got[k] for k in range(8)]
    other = send(jnp.concatenate(mine[1:], axis=0), fc=1)
    return mine + [partner] + [other[k * Q : (k + 1) * Q] for k in range(7)]


def gather_texts(own):
    near = send(own, dx=-1)
    far = send(own, dx=1)
    row = [own, near, send(own, dx=2), far]
    return row + [send(value, fy=3) for value in row]


def roll_to_place(table_rows, index):
    count = table_rows.shape[0]
    doubled = jnp.concatenate([table_rows, table_rows], axis=0)
    return lax.dynamic_slice_in_dim(doubled, (count - index) % count, count, 0)


def per_device(image_raw, text_raw, logit_scale_logarithm, logit_offset_bias):
    z, x = lax.axis_index("z"), lax.axis_index("x")
    yh, yl, core = lax.axis_index("yh"), lax.axis_index("yl"), lax.axis_index("core")
    y = yh * 2 + yl
    f32, f16 = jnp.float32, jnp.float16

    def quarter(block, l, c):
        return lax.dynamic_slice_in_dim(block, (l * 2 + c) * Q, Q, 0)

    image_unit, image_inv = normalize(quarter(image_raw, yl, core))
    partner_unit, _ = normalize(quarter(image_raw, yl, 1 - core))
    text_rows = jnp.concatenate([quarter(text_raw, yl, core), quarter(text_raw, 1 - yl, core)], axis=0)
    text_units, text_invs = normalize(text_rows)
    text_unit, text_inv = text_units[:Q], text_invs[:Q]
    temperature = jnp.exp(logit_scale_logarithm[0])
    params = jnp.stack([temperature, logit_offset_bias[0]])

    image_chunks = gather_images(image_unit.astype(jnp.bfloat16), partner_unit.astype(jnp.bfloat16))
    text_chunks = gather_texts(text_units.astype(jnp.bfloat16))
    gi, gt, li, lt, sums = pairs_on_device(params, image_chunks, text_chunks)

    half = gi[:512] + send(gi[512:].astype(f16), fc=1).astype(f32)
    gi_own = half[:Q]
    for k in range(1, 8):
        gi_own = gi_own + send(half[k * Q : (k + 1) * Q].astype(f16), dz=k).astype(f32)
    gt_own = gt[:Q]
    for f in range(2):
        for dx in range(4):
            for q in range(2):
                if dx or f or q:
                    start = ((f * 4 + dx) * 2 + q) * Q
                    flip = (0, 1, 3, 2)[f * 2 + q]
                    part = send(gt[start : start + Q].astype(f16), dx=dx, fy=flip)
                    gt_own = gt_own + part.astype(f32)

    grad_image = image_inv * (
        gi_own - image_unit * jnp.sum(image_unit * gi_own, axis=-1, keepdims=True)
    )
    grad_text = text_inv * (gt_own - text_unit * jnp.sum(text_unit * gt_own, axis=-1, keepdims=True))

    li = li.reshape(2, 8, Q)
    li = jnp.where(core == 0, li, li[::-1])
    li = roll_to_place(jnp.transpose(li, (1, 0, 2)).reshape(8, 2 * Q), z)
    lt = lt.reshape(2, 4, 2, Q)
    lt = jnp.stack([lt[0, :, 0], lt[0, :, 1], lt[1, :, 1], lt[1, :, 0]], axis=1)
    lt = jnp.where(yl == 0, lt, lt[:, jnp.array([1, 0, 3, 2])])
    lt = jnp.where(yh == 0, lt, lt[:, jnp.array([2, 3, 0, 1])])
    lt = roll_to_place(lt.reshape(4, 4 * Q), x)
    both = jnp.sum(sums, axis=1)
    pack_c = jnp.concatenate([li.reshape(-1), both])
    for move in (dict(fc=1), dict(fz=1), dict(fz=2), dict(fz=4)):
        pack_c = pack_c + send(pack_c, **move)
    pack_r = lt.reshape(-1)
    for move in (dict(fy=1), dict(fx=1), dict(fy=3), dict(fx=2)):
        pack_r = pack_r + send(pack_r, **move)
    both = pack_c[1024:]
    for move in (dict(fy=1), dict(fx=1), dict(fy=3), dict(fx=2)):
        both = both + send(both, **move)
    image_loss = lax.dynamic_slice_in_dim(pack_c, (z * 2 + core) * Q, Q, 0)
    text_loss = lax.dynamic_slice_in_dim(pack_r, (x * 4 + y) * Q, Q, 0)
    param_grads = jnp.stack([both[1], both[0]])
    return (grad_image, grad_text, image_loss, text_loss, param_grads)


def solution(mesh):
    fine = Mesh(mesh.devices.reshape(YH, NZ, NX, YL, NC), AXES)
    dp = ("yh", "z", "x")
    in_specs = (P(dp, None), P(dp, None), P(), P())
    out_specs = (P(AXES, None), P(AXES, None), P(AXES), P(AXES), P())
    return jax.shard_map(
        per_device, mesh=fine, in_specs=in_specs, out_specs=out_specs, check_vma=False
    )
```

```python
import jax
import jax.numpy as jnp
from jax import lax
from jax.experimental import pallas as pl
from jax.experimental.pallas import tpu as pltpu
from jax.sharding import Mesh, PartitionSpec as P

AXES = ("yh", "z", "x", "yl", "core")
YH, NZ, NX, YL, NC = 2, 8, 4, 2, 2
Q = 64


def table(move):
    pairs = []
    for yh in range(YH):
        for z in range(NZ):
            for x in range(NX):
                for yl in range(YL):
                    for c in range(NC):
                        y2, z2, x2, c2 = move(yh * 2 + yl, z, x, c)
                        y2, z2, x2 = y2 % 4, z2 % NZ, x2 % NX
                        source = (((yh * NZ + z) * NX + x) * YL + yl) * NC + c
                        target = (((y2 // 2 * NZ + z2) * NX + x2) * YL + y2 % 2) * NC + c2
                        pairs.append((source, target))
    return pairs


def send(value, dx=0, dz=0, fy=0, fz=0, fx=0, fc=0, split_z=0):
    pairs = table(
        lambda y, z, x, c: (y ^ fy, (z + dz + (1 - 2 * c) * split_z) ^ fz, (x + dx) ^ fx, c ^ fc)
    )
    return lax.ppermute(value, AXES, pairs)


def rounded(value):
    return lax.reduce_precision(value, 8, 7)


def normalize(embedding):
    floats = embedding.astype(jnp.float32)
    inverse = lax.rsqrt(jnp.sum(floats * floats, axis=-1, keepdims=True) + 1e-06)
    return (floats * inverse, inverse)


ROWS = 256


def pair_kernel(par_ref, *refs):
    a0, r1, r2, r3, r4, e12, e34 = refs[:7]
    txt_in = refs[7:15]
    gi_ref, gt_ref, li_ref, lt_ref, sums_ref, img, txt = refs[15:]
    z, x = lax.axis_index("z"), lax.axis_index("x")
    yh, core = lax.axis_index("yh"), lax.axis_index("core")
    sign = 1 - 2 * core
    img[0:64, :] = a0[pl.ds(pl.multiple_of(core * Q, Q), Q), :]
    img[64:320, :] = e12[...]
    img[320:448, :] = e34[0:128, :]
    img[448:512, :] = r4[...]
    img[512:576, :] = a0[pl.ds(pl.multiple_of((1 - core) * Q, Q), Q), :]
    img[576:704, :] = r1[...]
    img[704:832, :] = r2[...]
    img[832:960, :] = r3[...]
    img[960:1024, :] = e34[128:192, :]
    image_places = [(z, core)]
    image_places += [(z + sign * k, q) for k in range(1, 4) for q in range(2)]
    image_places += [(z + 4, core), (z, 1 - core)]
    image_places += [(z - sign * k, q) for k in range(1, 4) for q in range(2)]
    image_places += [(z + 4, 1 - core)]
    text_places = [
        (h * NX + lax.rem(x + dx, NX)) * 2 for h in (yh, 1 - yh) for dx in (0, NX - 1, 1, 2)
    ]
    own_column = (text_places[0] + lax.axis_index("yl")) * Q
    for k, ref in enumerate(txt_in):
        rows = ref.shape[0]
        txt[pl.ds(pl.multiple_of(text_places[k] * Q, Q), rows), :] = ref[...]
    temperature = par_ref[0]
    offset = par_ref[1]
    texts = txt[...]
    loss_cols = slope_sum = scale_sum = None
    for r in range(1024 // ROWS):
        images = img[r * ROWS : (r + 1) * ROWS, :]
        scores = lax.dot_general(
            images, texts, (((1,), (1,)), ((), ())), preferred_element_type=jnp.float32
        )
        p = jnp.exp(scores * temperature + offset)
        if r == 0:
            row = lax.broadcasted_iota(jnp.int32, (ROWS, 1024), 0)
            column = lax.broadcasted_iota(jnp.int32, (ROWS, 1024), 1)
            match = (column - row == own_column) & (row < Q)
            p = jnp.where(match, 0.0, p)
        q = 1.0 + p
        slopes = p / q
        losses = jnp.where(p < 0.0009765625, p - 0.5 * p * p, jnp.log(q))
        weights = (temperature * slopes).astype(jnp.bfloat16)
        gi_ref[r * ROWS : (r + 1) * ROWS, :] = jnp.dot(
            weights, texts, preferred_element_type=jnp.float32
        )
        back = lax.dot_general(
            weights, images, (((0,), (0,)), ((), ())), preferred_element_type=jnp.float32
        )
        row_losses = jnp.sum(losses, axis=1, keepdims=True)
        for k in range(ROWS // Q):
            zz, q = image_places[r * ROWS // Q + k]
            start = (q * NZ + lax.rem(zz + NZ, NZ)) * Q
            li_ref[pl.ds(pl.multiple_of(start, Q), Q), :] = row_losses[k * Q : (k + 1) * Q]
        cols = jnp.sum(losses, axis=0, keepdims=True)
        s1 = jnp.sum(slopes, axis=0, keepdims=True)
        s2 = jnp.sum(slopes * scores, axis=0, keepdims=True)
        if r == 0:
            gt_ref[...] = back
            loss_cols, slope_sum, scale_sum = cols, s1, s2
        else:
            gt_ref[...] += back
            loss_cols, slope_sum, scale_sum = loss_cols + cols, slope_sum + s1, scale_sum + s2
    lt_ref[...] = loss_cols
    sums_ref[0:1, :] = temperature * scale_sum
    sums_ref[1:2, :] = slope_sum


def pairs_on_device(params, chunks):
    width = chunks[0].shape[1]
    vmem = pl.BlockSpec(memory_space=pltpu.VMEM)
    smem = pl.BlockSpec(memory_space=pltpu.SMEM)
    f32 = jnp.float32
    return pl.pallas_call(
        pair_kernel,
        out_shape=(
            jax.ShapeDtypeStruct((1024, width), f32),
            jax.ShapeDtypeStruct((1024, width), f32),
            jax.ShapeDtypeStruct((1024, 1), f32),
            jax.ShapeDtypeStruct((1, 1024), f32),
            jax.ShapeDtypeStruct((2, 1024), f32),
        ),
        in_specs=[smem] + [vmem] * len(chunks),
        out_specs=(vmem,) * 5,
        scratch_shapes=[
            pltpu.VMEM((1024, width), jnp.bfloat16),
            pltpu.VMEM((1024, width), jnp.bfloat16),
        ],
        compiler_params=pltpu.CompilerParams(vmem_limit_bytes=48 * 1024 * 1024),
        cost_estimate=pl.CostEstimate(
            flops=6 * 1024 * 1024 * width, bytes_accessed=14 * 1024 * 1024, transcendentals=3 * 1024 * 1024
        ),
        name="pairs",
    )(params, *chunks)


def tied(*values):
    return lax.optimization_barrier(values)


def gather(a0, t0, core, own):
    r1 = send(a0, split_z=1)
    xm, xp, c0 = send(t0, dx=1), send(t0, dx=-1), send(t0, fy=3)
    a0, t0, r1, xm, xp, c0 = tied(a0, t0, r1, xm, xp, c0)
    r2 = send(r1, split_z=1)
    cm, cp = send(c0, dx=1), send(c0, dx=-1)
    f1, f2 = send(xm[:Q], dx=1), send(xp[Q:], dx=-1)
    r2, cm, cp, f1, f2, *own = tied(r2, cm, cp, f1, f2, *own)
    r3 = send(r2, split_z=1)
    g1, g2 = send(cm[:Q], dx=1), send(cp[Q:], dx=-1)
    e12 = send(jnp.concatenate([r1, r2], axis=0), fc=1)
    r3, g1, g2, e12 = tied(r3, g1, g2, e12)
    r4 = send(lax.dynamic_slice_in_dim(r3, core * Q, Q, 0), split_z=1)
    e34 = send(jnp.concatenate([r3, r4], axis=0), fc=1)
    far, far_h = jnp.concatenate([f1, f2], axis=0), jnp.concatenate([g1, g2], axis=0)
    return [a0, r1, r2, r3, r4, e12, e34, t0, xm, xp, far, c0, cm, cp, far_h], own


def per_device(image_raw, text_raw, logit_scale_logarithm, logit_offset_bias):
    z, x = lax.axis_index("z"), lax.axis_index("x")
    yh, yl, core = lax.axis_index("yh"), lax.axis_index("yl"), lax.axis_index("core")
    f32, f16, bf16 = jnp.float32, jnp.float16, jnp.bfloat16

    def quarter(block, l, c):
        return lax.dynamic_slice_in_dim(block, (l * 2 + c) * Q, Q, 0)

    a0 = normalize(lax.dynamic_slice_in_dim(image_raw, yl * 2 * Q, 2 * Q, 0))[0].astype(bf16)
    t0 = jnp.concatenate([quarter(text_raw, 0, core), quarter(text_raw, 1, core)], axis=0)
    t0 = normalize(t0)[0].astype(bf16)
    image_unit, image_inv = normalize(quarter(image_raw, yl, core))
    text_unit, text_inv = normalize(quarter(text_raw, yl, core))
    temperature, offset = jnp.exp(logit_scale_logarithm[0]), logit_offset_bias[0]
    params = jnp.stack([temperature, offset])

    image_low, text_low = rounded(image_unit), rounded(text_unit)
    match = jnp.sum(image_low * text_low, axis=-1)
    match_logit = temperature * match + offset
    match_loss = jnp.log1p(jnp.exp(-match_logit))
    match_slope = -1.0 / (1.0 + jnp.exp(match_logit))
    match_weight = rounded(temperature * match_slope)
    match_sums = jnp.stack([temperature * jnp.sum(match_slope * match), jnp.sum(match_slope)])
    own = (image_unit, text_unit, image_inv, text_inv, image_low, text_low, match_loss, match_weight, match_sums)
    chunks, own = gather(a0, t0, core, own)
    image_unit, text_unit, image_inv, text_inv, image_low, text_low, match_loss, match_weight, match_sums = own
    gi, gt, li, lt, sums = pairs_on_device(params, chunks)

    half = gi[:512] + send(gi[512:].astype(f16), fc=1).astype(f32)
    flight = half[Q:].astype(f16)
    far = send(flight[384:], dz=4)
    three, two, one = (send(flight[(k - 1) * 128 : k * 128], split_z=k) for k in (3, 2, 1))
    back_xy = lax.all_to_all(gt.astype(f16), ("yh", "x", "yl"), 0, 0, tiled=True)
    both = jnp.sum(sums, axis=1) + match_sums
    pack_c = jnp.concatenate([li.reshape(-1), both])
    for move in (dict(fc=1), dict(fz=1), dict(fz=2), dict(fz=4)):
        pack_c = pack_c + send(pack_c, **move)
    pack_r = lt.reshape(-1)
    for move in (dict(fy=1), dict(fx=1), dict(fy=3), dict(fx=2)):
        pack_r = pack_r + send(pack_r, **move)
    both = pack_c[1024:]
    for move in (dict(fy=1), dict(fx=1), dict(fy=3), dict(fx=2)):
        both = both + send(both, **move)
    far, three, two, one, pack_c, pack_r, both = tied(far, three, two, one, pack_c, pack_r, both)
    arrived = one.astype(f32) + two.astype(f32) + three.astype(f32)
    theirs = lax.dynamic_slice_in_dim(arrived, (1 - core) * Q, Q, 0)
    gi_own = half[:Q] + far.astype(f32) + lax.dynamic_slice_in_dim(arrived, core * Q, Q, 0)
    gi_own = gi_own + send(theirs, fc=1)
    gt_own = jnp.sum(back_xy.reshape(16, Q, -1).astype(f32), axis=0)

    gi_own = gi_own + match_weight[:, None] * text_low
    gt_own = gt_own + match_weight[:, None] * image_low
    grad_image = image_inv * (
        gi_own - image_unit * jnp.sum(image_unit * gi_own, axis=-1, keepdims=True)
    )
    grad_text = text_inv * (gt_own - text_unit * jnp.sum(text_unit * gt_own, axis=-1, keepdims=True))

    image_loss = lax.dynamic_slice_in_dim(pack_c, (core * 8 + z) * Q, Q, 0) + match_loss
    text_loss = lax.dynamic_slice_in_dim(pack_r, ((yh * 4 + x) * 2 + yl) * Q, Q, 0) + match_loss
    return (grad_image, grad_text, image_loss, text_loss, both)


def solution(mesh):
    fine = Mesh(mesh.devices.reshape(YH, NZ, NX, YL, NC), AXES)
    dp = ("yh", "z", "x")
    in_specs = (P(dp, None), P(dp, None), P(), P())
    out_specs = (P(AXES, None), P(AXES, None), P(AXES), P(AXES), P())
    return jax.shard_map(
        per_device, mesh=fine, in_specs=in_specs, out_specs=out_specs, check_vma=False
    )
```

```python
import jax
import jax.numpy as jnp
from jax import lax
from jax.experimental import pallas as pl
from jax.experimental.pallas import tpu as pltpu
from jax.sharding import Mesh, PartitionSpec as P

AXES = ("yh", "z", "x", "yl", "core")
YH, NZ, NX, YL, NC = 2, 8, 4, 2, 2
Q = 64


def table(move):
    pairs = []
    for yh in range(YH):
        for z in range(NZ):
            for x in range(NX):
                for yl in range(YL):
                    for c in range(NC):
                        y2, z2, x2, c2 = move(yh * 2 + yl, z, x, c)
                        y2, z2, x2 = y2 % 4, z2 % NZ, x2 % NX
                        source = (((yh * NZ + z) * NX + x) * YL + yl) * NC + c
                        target = (((y2 // 2 * NZ + z2) * NX + x2) * YL + y2 % 2) * NC + c2
                        pairs.append((source, target))
    return pairs


def send(value, dx=0, dz=0, fy=0, fz=0, fx=0, fc=0, split_z=0):
    pairs = table(
        lambda y, z, x, c: (y ^ fy, (z + dz + (1 - 2 * c) * split_z) ^ fz, (x + dx) ^ fx, c ^ fc)
    )
    return lax.ppermute(value, AXES, pairs)


def rounded(value):
    return lax.reduce_precision(value, 8, 7)


def normalize(embedding):
    floats = embedding.astype(jnp.float32)
    inverse = lax.rsqrt(jnp.sum(floats * floats, axis=-1, keepdims=True) + 1e-06)
    return (floats * inverse, inverse)


ROWS = 256


def pair_kernel(par_ref, *refs):
    all_images = refs[0]
    txt_in = refs[1:9]
    gi_ref, gt_ref, li_ref, lt_ref, sums_ref, img, txt = refs[9:]
    z, x = lax.axis_index("z"), lax.axis_index("x")
    yh, core = lax.axis_index("yh"), lax.axis_index("core")
    sign = 1 - 2 * core
    image_places = [(z, core)]
    image_places += [(z + sign * k, q) for k in range(1, 4) for q in range(2)]
    image_places += [(z + 4, core), (z, 1 - core)]
    image_places += [(z - sign * k, q) for k in range(1, 4) for q in range(2)]
    image_places += [(z + 4, 1 - core)]
    for k, (zz, q) in enumerate(image_places):
        start = (lax.rem(zz + NZ, NZ) * NC + q) * Q
        img[k * Q : (k + 1) * Q, :] = all_images[pl.ds(pl.multiple_of(start, Q), Q), :]
    text_places = [
        (h * NX + lax.rem(x + dx, NX)) * 2 for h in (yh, 1 - yh) for dx in (0, NX - 1, 1, 2)
    ]
    own_column = (text_places[0] + lax.axis_index("yl")) * Q
    for k, ref in enumerate(txt_in):
        rows = ref.shape[0]
        txt[pl.ds(pl.multiple_of(text_places[k] * Q, Q), rows), :] = ref[...]
    temperature = par_ref[0]
    offset = par_ref[1]
    texts = txt[...]
    loss_cols = slope_sum = scale_sum = None
    for r in range(1024 // ROWS):
        images = img[r * ROWS : (r + 1) * ROWS, :]
        scores = lax.dot_general(
            images, texts, (((1,), (1,)), ((), ())), preferred_element_type=jnp.float32
        )
        p = jnp.exp(scores * temperature + offset)
        if r == 0:
            row = lax.broadcasted_iota(jnp.int32, (ROWS, 1024), 0)
            column = lax.broadcasted_iota(jnp.int32, (ROWS, 1024), 1)
            match = (column - row == own_column) & (row < Q)
            p = jnp.where(match, 0.0, p)
        q = 1.0 + p
        slopes = p / q
        losses = jnp.where(p < 0.0009765625, p - 0.5 * p * p, jnp.log(q))
        weights = (temperature * slopes).astype(jnp.bfloat16)
        gi_ref[r * ROWS : (r + 1) * ROWS, :] = jnp.dot(
            weights, texts, preferred_element_type=jnp.float32
        )
        back = lax.dot_general(
            weights, images, (((0,), (0,)), ((), ())), preferred_element_type=jnp.float32
        )
        li_ref[r * ROWS : (r + 1) * ROWS, :] = jnp.sum(losses, axis=1, keepdims=True)
        cols = jnp.sum(losses, axis=0, keepdims=True)
        s1 = jnp.sum(slopes, axis=0, keepdims=True)
        s2 = jnp.sum(slopes * scores, axis=0, keepdims=True)
        if r == 0:
            gt_ref[...] = back
            loss_cols, slope_sum, scale_sum = cols, s1, s2
        else:
            gt_ref[...] += back
            loss_cols, slope_sum, scale_sum = loss_cols + cols, slope_sum + s1, scale_sum + s2
    lt_ref[...] = loss_cols
    sums_ref[0:1, :] = temperature * scale_sum
    sums_ref[1:2, :] = slope_sum


def pairs_on_device(params, chunks):
    width = chunks[0].shape[1]
    vmem = pl.BlockSpec(memory_space=pltpu.VMEM)
    smem = pl.BlockSpec(memory_space=pltpu.SMEM)
    f32 = jnp.float32
    return pl.pallas_call(
        pair_kernel,
        out_shape=(
            jax.ShapeDtypeStruct((1024, width), f32),
            jax.ShapeDtypeStruct((1024, width), f32),
            jax.ShapeDtypeStruct((1024, 1), f32),
            jax.ShapeDtypeStruct((1, 1024), f32),
            jax.ShapeDtypeStruct((2, 1024), f32),
        ),
        in_specs=[smem] + [vmem] * len(chunks),
        out_specs=(vmem,) * 5,
        scratch_shapes=[
            pltpu.VMEM((1024, width), jnp.bfloat16),
            pltpu.VMEM((1024, width), jnp.bfloat16),
        ],
        compiler_params=pltpu.CompilerParams(vmem_limit_bytes=48 * 1024 * 1024),
        cost_estimate=pl.CostEstimate(
            flops=6 * 1024 * 1024 * width, bytes_accessed=14 * 1024 * 1024, transcendentals=3 * 1024 * 1024
        ),
        name="pairs",
    )(params, *chunks)


def tied(*values):
    return lax.optimization_barrier(values)


def gather_texts(t0, own):
    xm, xp, c0 = send(t0, dx=1), send(t0, dx=-1), send(t0, fy=3)
    t0, xm, xp, c0 = tied(t0, xm, xp, c0)
    cm, cp = send(c0, dx=1), send(c0, dx=-1)
    f1, f2 = send(xm[:Q], dx=1), send(xp[Q:], dx=-1)
    cm, cp, f1, f2, *own = tied(cm, cp, f1, f2, *own)
    g1, g2 = send(cm[:Q], dx=1), send(cp[Q:], dx=-1)
    far = jnp.concatenate([f1, f2], axis=0)
    g1, g2, far = tied(g1, g2, far)
    return [t0, xm, xp, far, c0, cm, cp, jnp.concatenate([g1, g2], axis=0)], own


def per_device(image_raw, text_raw, logit_scale_logarithm, logit_offset_bias):
    z, x = lax.axis_index("z"), lax.axis_index("x")
    yh, yl, core = lax.axis_index("yh"), lax.axis_index("yl"), lax.axis_index("core")
    f32, f16, bf16 = jnp.float32, jnp.float16, jnp.bfloat16

    def quarter(block, l, c):
        return lax.dynamic_slice_in_dim(block, (l * 2 + c) * Q, Q, 0)

    t0 = jnp.concatenate([quarter(text_raw, 0, core), quarter(text_raw, 1, core)], axis=0)
    t0 = normalize(t0)[0].astype(bf16)
    image_unit, image_inv = normalize(quarter(image_raw, yl, core))
    all_images = lax.all_gather(image_unit.astype(bf16), ("z", "core"), tiled=True)
    text_unit, text_inv = normalize(quarter(text_raw, yl, core))
    temperature, offset = jnp.exp(logit_scale_logarithm[0]), logit_offset_bias[0]
    params = jnp.stack([temperature, offset])

    image_low, text_low = rounded(image_unit), rounded(text_unit)
    match = jnp.sum(image_low * text_low, axis=-1)
    match_logit = temperature * match + offset
    match_loss = jnp.log1p(jnp.exp(-match_logit))
    match_slope = -1.0 / (1.0 + jnp.exp(match_logit))
    match_weight = rounded(temperature * match_slope)
    match_sums = jnp.stack([temperature * jnp.sum(match_slope * match), jnp.sum(match_slope)])
    own = (image_unit, text_unit, image_inv, text_inv, image_low, text_low, match_loss, match_weight, match_sums)
    texts, own = gather_texts(t0, own)
    image_unit, text_unit, image_inv, text_inv, image_low, text_low, match_loss, match_weight, match_sums = own
    gi, gt, li, lt, sums = pairs_on_device(params, [all_images, *texts])

    li = li.reshape(-1)
    both = jnp.sum(sums, axis=1) + match_sums
    met = send(jnp.concatenate([li[512:], both]), fc=1)
    rows_met = send(gi[512:].astype(f16), fc=1)
    li_half, both = li[:512] + met[:512], both + met[512:]
    plane = jnp.concatenate([lt.reshape(-1), both])
    for move in (dict(fy=1), dict(fx=1), dict(fy=3), dict(fx=2)):
        plane = plane + send(plane, **move)
    place = (lax.broadcasted_iota(jnp.int32, (NZ, 2), 0) == z).astype(f32)
    here = (place * plane[None, 1024:]).reshape(-1)
    far_small = send(jnp.concatenate([li_half[448:], here]), dz=4)
    smalls = [
        send(jnp.concatenate([li_half[k * 128 - Q : k * 128 + Q], here]), split_z=k) for k in (1, 2, 3)
    ]
    half = gi[:512] + rows_met.astype(f32)
    flight = half[Q:].astype(f16)
    gt16 = gt.astype(f16)
    plane, gt16 = tied(plane, gt16)
    back_xy = lax.all_to_all(gt16, ("yh", "x", "yl"), 0, 0, tiled=True)
    far_small, one, two, three, flight = tied(far_small, *smalls, flight)
    small = one + two + three
    small_met = send(
        jnp.concatenate([lax.dynamic_slice_in_dim(small, (1 - core) * Q, Q, 0), small[128:]]), fc=1
    )
    image_loss = li_half[:Q] + far_small[:Q] + lax.dynamic_slice_in_dim(small, core * Q, Q, 0) + small_met[:Q]
    every_z = here + far_small[Q:] + small[128:] + small_met[Q:]
    both = jnp.sum(every_z.reshape(NZ, 2), axis=0)
    text_loss = lax.dynamic_slice_in_dim(plane, ((yh * 4 + x) * 2 + yl) * Q, Q, 0)
    far = send(flight[384:], dz=4)
    three, two, one = (send(flight[(k - 1) * 128 : k * 128], split_z=k) for k in (3, 2, 1))
    far, three, two, one, image_loss, both = tied(far, three, two, one, image_loss, both)
    arrived = one.astype(f32) + two.astype(f32) + three.astype(f32)
    theirs = lax.dynamic_slice_in_dim(arrived, (1 - core) * Q, Q, 0)
    gi_own = half[:Q] + far.astype(f32) + lax.dynamic_slice_in_dim(arrived, core * Q, Q, 0)
    gi_own = gi_own + send(theirs, fc=1)
    gt_own = jnp.sum(back_xy.reshape(16, Q, -1).astype(f32), axis=0)

    gi_own = gi_own + match_weight[:, None] * text_low
    gt_own = gt_own + match_weight[:, None] * image_low
    grad_image = image_inv * (
        gi_own - image_unit * jnp.sum(image_unit * gi_own, axis=-1, keepdims=True)
    )
    grad_text = text_inv * (gt_own - text_unit * jnp.sum(text_unit * gt_own, axis=-1, keepdims=True))

    image_loss, text_loss = image_loss + match_loss, text_loss + match_loss
    return (grad_image, grad_text, image_loss, text_loss, both)


def solution(mesh):
    fine = Mesh(mesh.devices.reshape(YH, NZ, NX, YL, NC), AXES)
    dp = ("yh", "z", "x")
    in_specs = (P(dp, None), P(dp, None), P(), P())
    out_specs = (P(AXES, None), P(AXES, None), P(AXES), P(AXES), P())
    return jax.shard_map(
        per_device, mesh=fine, in_specs=in_specs, out_specs=out_specs, check_vma=False
    )
```

```python
import jax
import jax.numpy as jnp
from jax import lax
from jax.experimental import pallas as pl
from jax.experimental.pallas import tpu as pltpu
from jax.sharding import Mesh, PartitionSpec as P

AXES = ("yh", "z", "x", "yl", "core")
YH, NZ, NX, YL, NC = 2, 8, 4, 2, 2
Q = 64


def table(move):
    pairs = []
    for yh in range(YH):
        for z in range(NZ):
            for x in range(NX):
                for yl in range(YL):
                    for c in range(NC):
                        y2, z2, x2, c2 = move(yh * 2 + yl, z, x, c)
                        y2, z2, x2 = y2 % 4, z2 % NZ, x2 % NX
                        source = (((yh * NZ + z) * NX + x) * YL + yl) * NC + c
                        target = (((y2 // 2 * NZ + z2) * NX + x2) * YL + y2 % 2) * NC + c2
                        pairs.append((source, target))
    return pairs


def send(value, dx=0, dz=0, fy=0, fz=0, fx=0, fc=0, split_z=0):
    pairs = table(
        lambda y, z, x, c: (y ^ fy, (z + dz + (1 - 2 * c) * split_z) ^ fz, (x + dx) ^ fx, c ^ fc)
    )
    return lax.ppermute(value, AXES, pairs)


def rounded(value):
    return lax.reduce_precision(value, 8, 7)


SUM_SCALE = 2.0**-14


def parts_of(values):
    high = lax.reduce_precision(values, 5, 10)
    return high, lax.reduce_precision(values - high, 5, 10)


def extra_rows(losses, sums, width):
    rows = [jnp.pad(v, (0, width - v.shape[0])) for v in (*losses, *sums)]
    return jnp.pad(jnp.stack(rows), ((0, 4), (0, 0))).astype(jnp.float16)


def normalize(embedding):
    floats = embedding.astype(jnp.float32)
    inverse = lax.rsqrt(jnp.sum(floats * floats, axis=-1, keepdims=True) + 1e-06)
    return (floats * inverse, inverse)


ROWS = 256


def pair_kernel(par_ref, *refs):
    a0, r1, r2, r3, r4, met = refs[:6]
    txt_in = refs[6:14]
    w_ref, img, txt, li_ref, lt_ref, sums_ref = refs[14:]
    x, yh, core = lax.axis_index("x"), lax.axis_index("yh"), lax.axis_index("core")
    img[0:64, :] = a0[pl.ds(pl.multiple_of(core * Q, Q), Q), :]
    img[64:448, :] = met[0:384, :]
    img[448:512, :] = r4[...]
    img[512:576, :] = a0[pl.ds(pl.multiple_of((1 - core) * Q, Q), Q), :]
    img[576:704, :] = r1[...]
    img[704:832, :] = r2[...]
    img[832:960, :] = r3[...]
    img[960:1024, :] = met[384:448, :]
    text_places = [
        (h * NX + lax.rem(x + dx, NX)) * 2 for h in (yh, 1 - yh) for dx in (0, NX - 1, 1, 2)
    ]
    own_column = (text_places[0] + lax.axis_index("yl")) * Q
    for k, ref in enumerate(txt_in):
        rows = ref.shape[0]
        txt[pl.ds(pl.multiple_of(text_places[k] * Q, Q), rows), :] = ref[...]
    temperature = par_ref[0]
    offset = par_ref[1]
    texts = txt[...]
    loss_cols = slope_sum = scale_sum = None
    for r in range(1024 // ROWS):
        images = img[r * ROWS : (r + 1) * ROWS, :]
        scores = lax.dot_general(
            images, texts, (((1,), (1,)), ((), ())), preferred_element_type=jnp.float32
        )
        p = jnp.exp(scores * temperature + offset)
        if r == 0:
            row = lax.broadcasted_iota(jnp.int32, (ROWS, 1024), 0)
            column = lax.broadcasted_iota(jnp.int32, (ROWS, 1024), 1)
            match = (column - row == own_column) & (row < Q)
            p = jnp.where(match, 0.0, p)
        q = 1.0 + p
        slopes = p / q
        losses = jnp.where(p < 0.0009765625, p - 0.5 * p * p, jnp.log(q))
        weights = (temperature * slopes).astype(jnp.bfloat16)
        w_ref[r * ROWS : (r + 1) * ROWS, :] = weights
        li_ref[r * ROWS : (r + 1) * ROWS, :] = jnp.sum(losses, axis=1, keepdims=True)
        cols = jnp.sum(losses, axis=0, keepdims=True)
        s1 = jnp.sum(slopes, axis=0, keepdims=True)
        s2 = jnp.sum(slopes * scores, axis=0, keepdims=True)
        if r == 0:
            loss_cols, slope_sum, scale_sum = cols, s1, s2
        else:
            loss_cols, slope_sum, scale_sum = loss_cols + cols, slope_sum + s1, scale_sum + s2
    lt_ref[...] = loss_cols
    sums_ref[0:1, :] = temperature * scale_sum
    sums_ref[1:2, :] = slope_sum


def pairs_on_device(params, chunks):
    width = chunks[0].shape[1]
    vmem = pl.BlockSpec(memory_space=pltpu.VMEM)
    smem = pl.BlockSpec(memory_space=pltpu.SMEM)
    f32 = jnp.float32
    return pl.pallas_call(
        pair_kernel,
        out_shape=(
            jax.ShapeDtypeStruct((1024, 1024), jnp.bfloat16),
            jax.ShapeDtypeStruct((1024, width), jnp.bfloat16),
            jax.ShapeDtypeStruct((1024, width), jnp.bfloat16),
            jax.ShapeDtypeStruct((1024, 1), f32),
            jax.ShapeDtypeStruct((1, 1024), f32),
            jax.ShapeDtypeStruct((2, 1024), f32),
        ),
        in_specs=[smem] + [vmem] * len(chunks),
        out_specs=(vmem,) * 6,
        compiler_params=pltpu.CompilerParams(vmem_limit_bytes=28 * 1024 * 1024),
        cost_estimate=pl.CostEstimate(
            flops=2 * 1024 * 1024 * width, bytes_accessed=12 * 1024 * 1024, transcendentals=3 * 1024 * 1024
        ),
        name="pairs",
    )(params, *chunks)


def tied(*values):
    return lax.optimization_barrier(values)


def gather(a0, t0, core, own):
    r3, r2 = send(a0, split_z=3), send(a0, split_z=2)
    xm, xp, c0 = send(t0, dx=1), send(t0, dx=-1), send(t0, fy=3)
    a0, t0, xm, xp, c0 = tied(a0, t0, xm, xp, c0)
    cm, cp = send(c0, dx=1), send(c0, dx=-1)
    f1, f2 = send(xm[:Q], dx=1), send(xp[Q:], dx=-1)
    a0, r3, r2, cm, cp, f1, f2, *own = tied(a0, r3, r2, cm, cp, f1, f2, *own)
    g1, g2 = send(cm[:Q], dx=1), send(cp[Q:], dx=-1)
    r1 = send(a0, split_z=1)
    r4 = send(lax.dynamic_slice_in_dim(a0, core * Q, Q, 0), dz=4)
    far = jnp.concatenate([f1, f2], axis=0)
    r1, r4, g1, g2, far = tied(r1, r4, g1, g2, far)
    met = send(jnp.concatenate([r1, r2, r3, r4], axis=0), fc=1)
    far_h = jnp.concatenate([g1, g2], axis=0)
    return [a0, r1, r2, r3, r4, met, t0, xm, xp, far, c0, cm, cp, far_h], own


def per_device(image_raw, text_raw, logit_scale_logarithm, logit_offset_bias):
    z, x = lax.axis_index("z"), lax.axis_index("x")
    width = image_raw.shape[1]
    yh, yl, core = lax.axis_index("yh"), lax.axis_index("yl"), lax.axis_index("core")
    f32, f16, bf16 = jnp.float32, jnp.float16, jnp.bfloat16

    def quarter(block, l, c):
        return lax.dynamic_slice_in_dim(block, (l * 2 + c) * Q, Q, 0)

    a0 = normalize(lax.dynamic_slice_in_dim(image_raw, yl * 2 * Q, 2 * Q, 0))[0].astype(bf16)
    t0 = jnp.concatenate([quarter(text_raw, 0, core), quarter(text_raw, 1, core)], axis=0)
    t0 = normalize(t0)[0].astype(bf16)
    image_unit, image_inv = normalize(quarter(image_raw, yl, core))
    text_unit, text_inv = normalize(quarter(text_raw, yl, core))
    temperature, offset = jnp.exp(logit_scale_logarithm[0]), logit_offset_bias[0]
    params = jnp.stack([temperature, offset])

    image_low, text_low = rounded(image_unit), rounded(text_unit)
    match = jnp.sum(image_low * text_low, axis=-1)
    match_logit = temperature * match + offset
    match_loss = jnp.log1p(jnp.exp(-match_logit))
    match_slope = -1.0 / (1.0 + jnp.exp(match_logit))
    match_weight = rounded(temperature * match_slope)
    match_sums = jnp.stack([temperature * jnp.sum(match_slope * match), jnp.sum(match_slope)])
    own = (image_unit, text_unit, image_inv, text_inv, image_low, text_low, match_loss, match_weight, match_sums)
    chunks, own = gather(a0, t0, core, own)
    image_unit, text_unit, image_inv, text_inv, image_low, text_low, match_loss, match_weight, match_sums = own
    weights, images, texts, li, lt, sums = pairs_on_device(params, chunks)

    li = li.reshape(-1)
    both = jnp.sum(sums, axis=1) + match_sums
    met = send(jnp.concatenate([li[512:], both]), fc=1)
    others = jnp.dot(weights[512:], texts, preferred_element_type=f32).astype(f16)
    met, others = tied(met, others)
    rows_met = send(others, fc=1)
    li_half, both = li[:512] + met[:512], both + met[512:]
    plane = jnp.concatenate([lt.reshape(-1), both])
    plane = plane + send(plane, fy=1)
    half = jnp.dot(weights[:512], texts, preferred_element_type=f32) + rows_met.astype(f32)
    flight = half[Q:].astype(f16)
    plane, half, flight = tied(plane, half, flight)
    plane = plane + send(plane, fx=1)
    gt16 = lax.dot_general(
        weights, images, (((0,), (0,)), ((), ())), preferred_element_type=f32
    ).astype(f16)
    plane, gt16 = tied(plane, gt16)
    for move in (dict(fy=3), dict(fx=2)):
        plane = plane + send(plane, **move)
    back_xy = lax.all_to_all(gt16, ("yh", "x", "yl"), 0, 0, tiled=True)
    text_loss = lax.dynamic_slice_in_dim(plane, ((yh * 4 + x) * 2 + yl) * Q, Q, 0)
    place = (lax.broadcasted_iota(jnp.int32, (NZ, 2), 0) == z).astype(f32)
    here = parts_of((place * plane[None, 1024:]).reshape(-1) * SUM_SCALE)
    far = send(jnp.concatenate([flight[384:], extra_rows(parts_of(li_half[448:]), here, width)]), dz=4)
    three, two, one = (
        send(
            jnp.concatenate(
                [
                    flight[(k - 1) * 128 : k * 128],
                    extra_rows(parts_of(li_half[k * 128 - Q : k * 128 + Q]), here, width),
                ]
            ),
            split_z=k,
        )
        for k in (3, 2, 1)
    )
    far, three, two, one = tied(far, three, two, one)
    arrived = one.astype(f32) + two.astype(f32) + three.astype(f32)
    theirs = jnp.concatenate([lax.dynamic_slice_in_dim(arrived, (1 - core) * Q, Q, 0), arrived[128:]])
    met = send(theirs, fc=1)
    gi_own = half[:Q] + far[:Q].astype(f32) + lax.dynamic_slice_in_dim(arrived, core * Q, Q, 0) + met[:Q]

    def own_losses(rows):
        return lax.dynamic_slice_in_dim(rows[0, :128] + rows[1, :128], core * Q, Q, 0)

    far_rows = far[Q:].astype(f32)
    image_loss = li_half[:Q] + far_rows[0, :Q] + far_rows[1, :Q] + own_losses(arrived[128:]) + own_losses(met[Q:])
    every_z = far_rows[2:4, : 2 * NZ] + arrived[130:132, : 2 * NZ] + met[Q + 2 : Q + 4, : 2 * NZ] + jnp.stack(here)
    both = jnp.sum((every_z[0] + every_z[1]).reshape(NZ, 2), axis=0) / SUM_SCALE
    gt_own = jnp.sum(back_xy.reshape(16, Q, -1).astype(f32), axis=0)

    gi_own = gi_own + match_weight[:, None] * text_low
    gt_own = gt_own + match_weight[:, None] * image_low
    grad_image = image_inv * (
        gi_own - image_unit * jnp.sum(image_unit * gi_own, axis=-1, keepdims=True)
    )
    grad_text = text_inv * (gt_own - text_unit * jnp.sum(text_unit * gt_own, axis=-1, keepdims=True))

    image_loss, text_loss = image_loss + match_loss, text_loss + match_loss
    return (grad_image, grad_text, image_loss, text_loss, both)


def solution(mesh):
    fine = Mesh(mesh.devices.reshape(YH, NZ, NX, YL, NC), AXES)
    dp = ("yh", "z", "x")
    in_specs = (P(dp, None), P(dp, None), P(), P())
    out_specs = (P(AXES, None), P(AXES, None), P(AXES), P(AXES), P())
    return jax.shard_map(
        per_device, mesh=fine, in_specs=in_specs, out_specs=out_specs, check_vma=False
    )
```

```python
import jax
import jax.numpy as jnp
from jax import lax
from jax.experimental import pallas as pl
from jax.experimental.pallas import tpu as pltpu
from jax.sharding import Mesh, PartitionSpec as P

AXES = ("yh", "z", "x", "yl", "core")
YH, NZ, NX, YL, NC = 2, 8, 4, 2, 2
Q = 64


def table(move):
    pairs = []
    for yh in range(YH):
        for z in range(NZ):
            for x in range(NX):
                for yl in range(YL):
                    for c in range(NC):
                        y2, z2, x2, c2 = move(yh * 2 + yl, z, x, c)
                        y2, z2, x2 = y2 % 4, z2 % NZ, x2 % NX
                        source = (((yh * NZ + z) * NX + x) * YL + yl) * NC + c
                        target = (((y2 // 2 * NZ + z2) * NX + x2) * YL + y2 % 2) * NC + c2
                        pairs.append((source, target))
    return pairs


def send(value, dx=0, dz=0, fy=0, fz=0, fx=0, fc=0, split_z=0):
    pairs = table(
        lambda y, z, x, c: (y ^ fy, (z + dz + (1 - 2 * c) * split_z) ^ fz, (x + dx) ^ fx, c ^ fc)
    )
    return lax.ppermute(value, AXES, pairs)


def rounded(value):
    return lax.reduce_precision(value, 8, 7)


SUM_SCALE = 2.0**-14


def parts_of(values):
    high = lax.reduce_precision(values, 5, 10)
    return high, lax.reduce_precision(values - high, 5, 10)


def extra_rows(losses, sums, width):
    rows = [jnp.pad(v, (0, width - v.shape[0])) for v in (*losses, *sums)]
    return jnp.pad(jnp.stack(rows), ((0, 4), (0, 0))).astype(jnp.float16)


def normalize(embedding):
    floats = embedding.astype(jnp.float32)
    inverse = lax.rsqrt(jnp.sum(floats * floats, axis=-1, keepdims=True) + 1e-06)
    return (floats * inverse, inverse)


ROWS = 256


def pair_kernel(par_ref, *refs):
    a0, r1, r2, r3, r4, met = refs[:6]
    txt_in = refs[6:14]
    w_out, img_out, txt_out, li_ref, lt_ref, sums_ref, w_ref, img, txt, sems = refs[14:]
    x, yh, core = lax.axis_index("x"), lax.axis_index("yh"), lax.axis_index("core")
    img[0:64, :] = a0[pl.ds(pl.multiple_of(core * Q, Q), Q), :]
    img[64:448, :] = met[0:384, :]
    img[448:512, :] = r4[...]
    img[512:576, :] = a0[pl.ds(pl.multiple_of((1 - core) * Q, Q), Q), :]
    img[576:704, :] = r1[...]
    img[704:832, :] = r2[...]
    img[832:960, :] = r3[...]
    img[960:1024, :] = met[384:448, :]
    text_places = [
        (h * NX + lax.rem(x + dx, NX)) * 2 for h in (yh, 1 - yh) for dx in (0, NX - 1, 1, 2)
    ]
    own_column = (text_places[0] + lax.axis_index("yl")) * Q
    for k, ref in enumerate(txt_in):
        rows = ref.shape[0]
        txt[pl.ds(pl.multiple_of(text_places[k] * Q, Q), rows), :] = ref[...]
    copies = [pltpu.make_async_copy(txt, txt_out, sems.at[0]), pltpu.make_async_copy(img, img_out, sems.at[1])]
    for copy in copies:
        copy.start()
    temperature = par_ref[0]
    offset = par_ref[1]
    texts = txt[...]
    loss_cols = slope_sum = scale_sum = None
    for r in range(1024 // ROWS):
        images = img[r * ROWS : (r + 1) * ROWS, :]
        scores = lax.dot_general(
            images, texts, (((1,), (1,)), ((), ())), preferred_element_type=jnp.float32
        )
        p = jnp.exp(scores * temperature + offset)
        if r == 0:
            row = lax.broadcasted_iota(jnp.int32, (ROWS, 1024), 0)
            column = lax.broadcasted_iota(jnp.int32, (ROWS, 1024), 1)
            match = (column - row == own_column) & (row < Q)
            p = jnp.where(match, 0.0, p)
        q = 1.0 + p
        slopes = p / q
        losses = jnp.where(p < 0.0009765625, p - 0.5 * p * p, jnp.log(q))
        weights = (temperature * slopes).astype(jnp.bfloat16)
        band = pl.ds(r * ROWS, ROWS)
        w_ref[band, :] = weights
        copy = pltpu.make_async_copy(w_ref.at[band], w_out.at[band], sems.at[2 + r])
        copy.start()
        copies.append(copy)
        li_ref[r * ROWS : (r + 1) * ROWS, :] = jnp.sum(losses, axis=1, keepdims=True)
        cols = jnp.sum(losses, axis=0, keepdims=True)
        s1 = jnp.sum(slopes, axis=0, keepdims=True)
        s2 = jnp.sum(slopes * scores, axis=0, keepdims=True)
        if r == 0:
            loss_cols, slope_sum, scale_sum = cols, s1, s2
        else:
            loss_cols, slope_sum, scale_sum = loss_cols + cols, slope_sum + s1, scale_sum + s2
    lt_ref[...] = loss_cols
    sums_ref[0:1, :] = temperature * scale_sum
    sums_ref[1:2, :] = slope_sum
    for copy in copies:
        copy.wait()


def pairs_on_device(params, chunks):
    width = chunks[0].shape[1]
    vmem = pl.BlockSpec(memory_space=pltpu.VMEM)
    smem = pl.BlockSpec(memory_space=pltpu.SMEM)
    f32 = jnp.float32
    return pl.pallas_call(
        pair_kernel,
        out_shape=(
            jax.ShapeDtypeStruct((1024, 1024), jnp.bfloat16),
            jax.ShapeDtypeStruct((1024, width), jnp.bfloat16),
            jax.ShapeDtypeStruct((1024, width), jnp.bfloat16),
            jax.ShapeDtypeStruct((1024, 1), f32),
            jax.ShapeDtypeStruct((1, 1024), f32),
            jax.ShapeDtypeStruct((2, 1024), f32),
        ),
        in_specs=[smem] + [vmem] * len(chunks),
        out_specs=(pl.BlockSpec(memory_space=pltpu.HBM),) * 3 + (vmem,) * 3,
        scratch_shapes=[
            pltpu.VMEM((1024, 1024), jnp.bfloat16),
            pltpu.VMEM((1024, width), jnp.bfloat16),
            pltpu.VMEM((1024, width), jnp.bfloat16),
            pltpu.SemaphoreType.DMA((6,)),
        ],
        compiler_params=pltpu.CompilerParams(vmem_limit_bytes=28 * 1024 * 1024),
        cost_estimate=pl.CostEstimate(
            flops=2 * 1024 * 1024 * width, bytes_accessed=12 * 1024 * 1024, transcendentals=3 * 1024 * 1024
        ),
        name="pairs",
    )(params, *chunks)


def finish_kernel(
    half, far, arrived, met, gt, image_unit, text_unit, image_inv, text_inv, weight, loss, here, gi_out, gt_out, loss_out, both_out
):
    core = lax.axis_index("core")
    own = arrived[pl.ds(pl.multiple_of(core * Q, Q), Q), :]
    gi = half[...] + far[0:Q, :] + own + met[0:Q, :]
    images, texts, w = image_unit[...], text_unit[...], weight[...]
    gi = gi + w * texts.astype(jnp.bfloat16).astype(jnp.float32)
    gi_out[...] = image_inv[...] * (gi - images * jnp.sum(images * gi, axis=-1, keepdims=True))
    gt = gt[...] + w * images.astype(jnp.bfloat16).astype(jnp.float32)
    gt_out[...] = text_inv[...] * (gt - texts * jnp.sum(texts * gt, axis=-1, keepdims=True))
    near = arrived[128:130, 0:128] + met[Q : Q + 2, 0:128]
    near = jnp.where(core == 0, near[:, :Q], near[:, Q:]) + far[Q : Q + 2, 0:Q]
    loss_out[...] = loss[...] + near[0:1] + near[1:2]
    sums = arrived[130:132, 0:128] + met[Q + 2 : Q + 4, 0:128] + far[Q + 2 : Q + 4, 0:128] + here[...]
    sums = sums[0:1] + sums[1:2]
    total = sums[:, 0:2]
    for k in range(1, NZ):
        total = total + sums[:, 2 * k : 2 * k + 2]
    both_out[...] = total * (1.0 / SUM_SCALE)


def finish(*args):
    width = args[0].shape[1]
    shape = jax.ShapeDtypeStruct((Q, width), jnp.float32)
    return pl.pallas_call(
        finish_kernel,
        out_shape=(
            shape,
            shape,
            jax.ShapeDtypeStruct((1, Q), jnp.float32),
            jax.ShapeDtypeStruct((1, 2), jnp.float32),
        ),
        compiler_params=pltpu.CompilerParams(vmem_limit_bytes=12 * 1024 * 1024),
        name="finish",
    )(*args)


def tied(*values):
    return lax.optimization_barrier(values)


def gather(a0, t0, core, own):
    r4 = send(lax.dynamic_slice_in_dim(a0, core * Q, Q, 0), dz=4)
    r3 = send(a0, split_z=3)
    xm, xp, c0 = send(t0, dx=1), send(t0, dx=-1), send(t0, fy=3)
    a0, t0, xm, xp, c0 = tied(a0, t0, xm, xp, c0)
    cm, cp = send(c0, dx=1), send(c0, dx=-1)
    f1, f2 = send(xm[:Q], dx=1), send(xp[Q:], dx=-1)
    r2 = send(a0, split_z=2)
    a0, r3, r4, cm, cp, f1, f2, *own = tied(a0, r3, r4, cm, cp, f1, f2, *own)
    g1, g2 = send(cm[:Q], dx=1), send(cp[Q:], dx=-1)
    r1 = send(a0, split_z=1)
    far = jnp.concatenate([f1, f2], axis=0)
    r1, r2, g1, g2, far = tied(r1, r2, g1, g2, far)
    met = send(jnp.concatenate([r1, r2, r3, r4], axis=0), fc=1)
    far_h = jnp.concatenate([g1, g2], axis=0)
    return [a0, r1, r2, r3, r4, met, t0, xm, xp, far, c0, cm, cp, far_h], own


def per_device(image_raw, text_raw, logit_scale_logarithm, logit_offset_bias):
    z, x = lax.axis_index("z"), lax.axis_index("x")
    width = image_raw.shape[1]
    yh, yl, core = lax.axis_index("yh"), lax.axis_index("yl"), lax.axis_index("core")
    f32, f16, bf16 = jnp.float32, jnp.float16, jnp.bfloat16

    def quarter(block, l, c):
        return lax.dynamic_slice_in_dim(block, (l * 2 + c) * Q, Q, 0)

    a0 = normalize(lax.dynamic_slice_in_dim(image_raw, yl * 2 * Q, 2 * Q, 0))[0].astype(bf16)
    t0 = jnp.concatenate([quarter(text_raw, 0, core), quarter(text_raw, 1, core)], axis=0)
    t0 = normalize(t0)[0].astype(bf16)
    image_unit, image_inv = normalize(quarter(image_raw, yl, core))
    text_unit, text_inv = normalize(quarter(text_raw, yl, core))
    temperature, offset = jnp.exp(logit_scale_logarithm[0]), logit_offset_bias[0]
    params = jnp.stack([temperature, offset])

    image_low, text_low = rounded(image_unit), rounded(text_unit)
    match = jnp.sum(image_low * text_low, axis=-1)
    match_logit = temperature * match + offset
    match_loss = jnp.log1p(jnp.exp(-match_logit))
    match_slope = -1.0 / (1.0 + jnp.exp(match_logit))
    match_weight = rounded(temperature * match_slope)
    match_sums = jnp.stack([temperature * jnp.sum(match_slope * match), jnp.sum(match_slope)])
    own = (image_unit, text_unit, image_inv, text_inv, match_loss, match_weight, match_sums)
    chunks, own = gather(a0, t0, core, own)
    image_unit, text_unit, image_inv, text_inv, match_loss, match_weight, match_sums = own
    weights, images, texts, li, lt, sums = pairs_on_device(params, chunks)

    li = li.reshape(-1)
    both = jnp.sum(sums, axis=1) + match_sums
    met = send(jnp.concatenate([li[512:], both]), fc=1)
    met, weights = tied(met, weights)
    li_half, both = li[:512] + met[:512], both + met[512:]
    plane = jnp.concatenate([lt.reshape(-1), both])
    plane = plane + send(plane, fy=1)
    others = jnp.dot(weights[512:], texts, preferred_element_type=f32).astype(f16)
    plane, others = tied(plane, others)
    plane = plane + send(plane, fx=1)
    rows_met = send(others, fc=1)
    gt16 = lax.dot_general(
        weights, images, (((0,), (0,)), ((), ())), preferred_element_type=f32
    ).astype(f16)
    plane, gt16, rows_met = tied(plane, gt16, rows_met)
    plane = plane + send(plane, fy=3)
    half = jnp.dot(weights[:512], texts, preferred_element_type=f32) + rows_met.astype(f32)
    flight = half[Q:].astype(f16)
    plane, gt16, half, flight = tied(plane, gt16, half, flight)
    plane = plane + send(plane, fx=2)
    back_xy = lax.all_to_all(gt16, ("yh", "x", "yl"), 0, 0, tiled=True)
    text_loss = lax.dynamic_slice_in_dim(plane, ((yh * 4 + x) * 2 + yl) * Q, Q, 0)
    place = (lax.broadcasted_iota(jnp.int32, (NZ, 2), 0) == z).astype(f32)
    here = parts_of((place * plane[None, 1024:]).reshape(-1) * SUM_SCALE)
    far = send(jnp.concatenate([flight[384:], extra_rows(parts_of(li_half[448:]), here, width)]), dz=4)
    three, two, one = (
        send(
            jnp.concatenate(
                [
                    flight[(k - 1) * 128 : k * 128],
                    extra_rows(parts_of(li_half[k * 128 - Q : k * 128 + Q]), here, width),
                ]
            ),
            split_z=k,
        )
        for k in (3, 2, 1)
    )
    far, three, two, one = tied(far, three, two, one)
    arrived = one.astype(f32) + two.astype(f32) + three.astype(f32)
    theirs = jnp.concatenate([lax.dynamic_slice_in_dim(arrived, (1 - core) * Q, Q, 0), arrived[128:]])
    met = send(theirs, fc=1)
    gt_own = jnp.sum(back_xy.reshape(16, Q, -1).astype(f32), axis=0)
    here_row = jnp.pad(jnp.stack(here), ((0, 0), (0, 128 - 2 * NZ)))
    grad_image, grad_text, image_loss, both = finish(
        half[:Q], far.astype(f32), arrived, met, gt_own, image_unit, text_unit, image_inv, text_inv,
        match_weight[:, None], (li_half[:Q] + match_loss)[None], here_row,
    )
    image_loss, both, text_loss = image_loss.reshape(Q), both.reshape(2), text_loss + match_loss
    return (grad_image, grad_text, image_loss, text_loss, both)


def solution(mesh):
    fine = Mesh(mesh.devices.reshape(YH, NZ, NX, YL, NC), AXES)
    dp = ("yh", "z", "x")
    in_specs = (P(dp, None), P(dp, None), P(), P())
    out_specs = (P(AXES, None), P(AXES, None), P(AXES), P(AXES), P())
    return jax.shard_map(
        per_device, mesh=fine, in_specs=in_specs, out_specs=out_specs, check_vma=False
    )
```

```python
import jax
import jax.numpy as jnp
from jax import lax
from jax.experimental import pallas as pl
from jax.experimental.pallas import tpu as pltpu
from jax.sharding import Mesh, PartitionSpec as P

AXES = ("yh", "z", "x", "yl", "core")
YH, NZ, NX, YL, NC = 2, 8, 4, 2, 2
Q = 64


def table(move):
    pairs = []
    for yh in range(YH):
        for z in range(NZ):
            for x in range(NX):
                for yl in range(YL):
                    for c in range(NC):
                        y2, z2, x2, c2 = move(yh * 2 + yl, z, x, c)
                        y2, z2, x2 = y2 % 4, z2 % NZ, x2 % NX
                        source = (((yh * NZ + z) * NX + x) * YL + yl) * NC + c
                        target = (((y2 // 2 * NZ + z2) * NX + x2) * YL + y2 % 2) * NC + c2
                        pairs.append((source, target))
    return pairs


def send(value, dx=0, dz=0, fy=0, fz=0, fx=0, fc=0, split_z=0):
    pairs = table(
        lambda y, z, x, c: (y ^ fy, (z + dz + (1 - 2 * c) * split_z) ^ fz, (x + dx) ^ fx, c ^ fc)
    )
    return lax.ppermute(value, AXES, pairs)


def rounded(value):
    return lax.reduce_precision(value, 8, 7)


SUM_SCALE = 2.0**-14


def parts_of(values):
    high = lax.reduce_precision(values, 5, 10)
    return high, lax.reduce_precision(values - high, 5, 10)


def two_rows(parts, width):
    return jnp.pad(jnp.stack(parts), ((0, 0), (0, width - parts[0].shape[0]))).astype(jnp.float16)


def extra_rows(losses, sums):
    return jnp.concatenate([losses, sums, jnp.zeros((4, losses.shape[1]), jnp.float16)])


def normalize(embedding):
    floats = embedding.astype(jnp.float32)
    inverse = lax.rsqrt(jnp.sum(floats * floats, axis=-1, keepdims=True) + 1e-06)
    return (floats * inverse, inverse)


ROWS = 256


def pair_kernel(par_ref, *refs):
    a0, r1, r2, r3, r4, met = refs[:6]
    txt_in = refs[6:14]
    w_out, img_out, txt_out, li_ref, lt_ref, sums_ref, w_ref, img, txt, sems = refs[14:]
    x, yh, core = lax.axis_index("x"), lax.axis_index("yh"), lax.axis_index("core")
    img[0:64, :] = a0[pl.ds(pl.multiple_of(core * Q, Q), Q), :]
    img[64:448, :] = met[0:384, :]
    img[448:512, :] = r4[...]
    img[512:576, :] = a0[pl.ds(pl.multiple_of((1 - core) * Q, Q), Q), :]
    img[576:704, :] = r1[...]
    img[704:832, :] = r2[...]
    img[832:960, :] = r3[...]
    img[960:1024, :] = met[384:448, :]
    text_places = [
        (h * NX + lax.rem(x + dx, NX)) * 2 for h in (yh, 1 - yh) for dx in (0, NX - 1, 1, 2)
    ]
    own_column = (text_places[0] + lax.axis_index("yl")) * Q
    for k, ref in enumerate(txt_in):
        rows = ref.shape[0]
        txt[pl.ds(pl.multiple_of(text_places[k] * Q, Q), rows), :] = ref[...]
    copies = [pltpu.make_async_copy(txt, txt_out, sems.at[0]), pltpu.make_async_copy(img, img_out, sems.at[1])]
    for copy in copies:
        copy.start()
    temperature = par_ref[0]
    offset = par_ref[1]
    texts = txt[...]
    loss_cols = slope_sum = scale_sum = None
    for r in range(1024 // ROWS):
        images = img[r * ROWS : (r + 1) * ROWS, :]
        scores = lax.dot_general(
            images, texts, (((1,), (1,)), ((), ())), preferred_element_type=jnp.float32
        )
        p = jnp.exp(scores * temperature + offset)
        if r == 0:
            row = lax.broadcasted_iota(jnp.int32, (ROWS, 1024), 0)
            column = lax.broadcasted_iota(jnp.int32, (ROWS, 1024), 1)
            match = (column - row == own_column) & (row < Q)
            p = jnp.where(match, 0.0, p)
        q = 1.0 + p
        slopes = p / q
        losses = jnp.where(p < 0.0009765625, p - 0.5 * p * p, jnp.log(q))
        weights = (temperature * slopes).astype(jnp.bfloat16)
        band = pl.ds(r * ROWS, ROWS)
        w_ref[band, :] = weights
        copy = pltpu.make_async_copy(w_ref.at[band], w_out.at[band], sems.at[2 + r])
        copy.start()
        copies.append(copy)
        li_ref[r * ROWS : (r + 1) * ROWS, :] = jnp.sum(losses, axis=1, keepdims=True)
        cols = jnp.sum(losses, axis=0, keepdims=True)
        s1 = jnp.sum(slopes, axis=0, keepdims=True)
        s2 = jnp.sum(slopes * scores, axis=0, keepdims=True)
        if r == 0:
            loss_cols, slope_sum, scale_sum = cols, s1, s2
        else:
            loss_cols, slope_sum, scale_sum = loss_cols + cols, slope_sum + s1, scale_sum + s2
    lt_ref[...] = loss_cols
    sums_ref[0:1, :] = temperature * scale_sum
    sums_ref[1:2, :] = slope_sum
    for copy in copies:
        copy.wait()


def pairs_on_device(params, chunks):
    width = chunks[0].shape[1]
    vmem = pl.BlockSpec(memory_space=pltpu.VMEM)
    smem = pl.BlockSpec(memory_space=pltpu.SMEM)
    f32 = jnp.float32
    return pl.pallas_call(
        pair_kernel,
        out_shape=(
            pltpu.HBM((1024, 1024), jnp.bfloat16),
            pltpu.HBM((1024, width), jnp.bfloat16),
            pltpu.HBM((1024, width), jnp.bfloat16),
            jax.ShapeDtypeStruct((1024, 1), f32),
            jax.ShapeDtypeStruct((1, 1024), f32),
            jax.ShapeDtypeStruct((2, 1024), f32),
        ),
        in_specs=[smem] + [vmem] * len(chunks),
        out_specs=(pl.BlockSpec(memory_space=pltpu.HBM),) * 3 + (vmem,) * 3,
        scratch_shapes=[
            pltpu.VMEM((1024, 1024), jnp.bfloat16),
            pltpu.VMEM((1024, width), jnp.bfloat16),
            pltpu.VMEM((1024, width), jnp.bfloat16),
            pltpu.SemaphoreType.DMA((6,)),
        ],
        compiler_params=pltpu.CompilerParams(vmem_limit_bytes=28 * 1024 * 1024),
        cost_estimate=pl.CostEstimate(
            flops=2 * 1024 * 1024 * width, bytes_accessed=12 * 1024 * 1024, transcendentals=3 * 1024 * 1024
        ),
        name="pairs",
    )(params, *chunks)


def finish_kernel(
    half, far, arrived, met, gt, image_unit, text_unit, image_inv, text_inv, weight, loss, here, gi_out, gt_out, loss_out, both_out
):
    core = lax.axis_index("core")
    own = arrived[pl.ds(pl.multiple_of(core * Q, Q), Q), :]
    gi = half[...] + far[0:Q, :] + own + met[0:Q, :]
    images, texts, w = image_unit[...], text_unit[...], weight[...]
    gi = gi + w * texts.astype(jnp.bfloat16).astype(jnp.float32)
    gi_out[...] = image_inv[...] * (gi - images * jnp.sum(images * gi, axis=-1, keepdims=True))
    gt = gt[...] + w * images.astype(jnp.bfloat16).astype(jnp.float32)
    gt_out[...] = text_inv[...] * (gt - texts * jnp.sum(texts * gt, axis=-1, keepdims=True))
    near = arrived[128:130, 0:128] + met[Q : Q + 2, 0:128]
    near = jnp.where(core == 0, near[:, :Q], near[:, Q:]) + far[Q : Q + 2, 0:Q]
    loss_out[...] = loss[...] + near[0:1] + near[1:2]
    sums = arrived[130:132, 0:128] + met[Q + 2 : Q + 4, 0:128] + far[Q + 2 : Q + 4, 0:128] + here[...]
    sums = sums[0:1] + sums[1:2]
    total = sums[:, 0:2]
    for k in range(1, NZ):
        total = total + sums[:, 2 * k : 2 * k + 2]
    both_out[...] = total * (1.0 / SUM_SCALE)


def finish(*args):
    width = args[0].shape[1]
    shape = jax.ShapeDtypeStruct((Q, width), jnp.float32)
    return pl.pallas_call(
        finish_kernel,
        out_shape=(
            shape,
            shape,
            jax.ShapeDtypeStruct((1, Q), jnp.float32),
            jax.ShapeDtypeStruct((1, 2), jnp.float32),
        ),
        compiler_params=pltpu.CompilerParams(vmem_limit_bytes=12 * 1024 * 1024),
        name="finish",
    )(*args)


def tied(*values):
    return lax.optimization_barrier(values)


def gather(a0, t0, core, own):
    r1 = send(a0, split_z=1)
    r4 = send(lax.dynamic_slice_in_dim(a0, core * Q, Q, 0), dz=4)
    xm, xp, c0 = send(t0, dx=1), send(t0, dx=-1), send(t0, fy=3)
    r1, t0, xm, xp, c0 = tied(r1, t0, xm, xp, c0)
    r3, r2 = send(r1, split_z=2), send(r1, split_z=1)
    cm, cp = send(c0, dx=1), send(c0, dx=-1)
    f1, f2 = send(xm[:Q], dx=1), send(xp[Q:], dx=-1)
    r2, r3, r4, cm, cp, f1, f2, *own = tied(r2, r3, r4, cm, cp, f1, f2, *own)
    g1, g2 = send(cm[:Q], dx=1), send(cp[Q:], dx=-1)
    met = send(jnp.concatenate([r1, r2, r3, r4], axis=0), fc=1)
    far = jnp.concatenate([f1, f2], axis=0)
    far_h = jnp.concatenate([g1, g2], axis=0)
    return [a0, r1, r2, r3, r4, met, t0, xm, xp, far, c0, cm, cp, far_h], own


def per_device(image_raw, text_raw, logit_scale_logarithm, logit_offset_bias):
    z, x = lax.axis_index("z"), lax.axis_index("x")
    width = image_raw.shape[1]
    yh, yl, core = lax.axis_index("yh"), lax.axis_index("yl"), lax.axis_index("core")
    f32, f16, bf16 = jnp.float32, jnp.float16, jnp.bfloat16

    def quarter(block, l, c):
        return lax.dynamic_slice_in_dim(block, (l * 2 + c) * Q, Q, 0)

    a0 = normalize(lax.dynamic_slice_in_dim(image_raw, yl * 2 * Q, 2 * Q, 0))[0].astype(bf16)
    t0 = jnp.concatenate([quarter(text_raw, 0, core), quarter(text_raw, 1, core)], axis=0)
    t0 = normalize(t0)[0].astype(bf16)
    image_unit, image_inv = normalize(quarter(image_raw, yl, core))
    text_unit, text_inv = normalize(quarter(text_raw, yl, core))
    temperature, offset = jnp.exp(logit_scale_logarithm[0]), logit_offset_bias[0]
    params = jnp.stack([temperature, offset])

    image_low, text_low = rounded(image_unit), rounded(text_unit)
    match = jnp.sum(image_low * text_low, axis=-1)
    match_logit = temperature * match + offset
    match_loss = jnp.log1p(jnp.exp(-match_logit))
    match_slope = -1.0 / (1.0 + jnp.exp(match_logit))
    match_weight = rounded(temperature * match_slope)
    match_sums = jnp.stack([temperature * jnp.sum(match_slope * match), jnp.sum(match_slope)])
    own = (image_unit, text_unit, image_inv, text_inv, match_loss, match_weight, match_sums)
    chunks, own = gather(a0, t0, core, own)
    image_unit, text_unit, image_inv, text_inv, match_loss, match_weight, match_sums = own
    weights, images, texts, li, lt, sums = pairs_on_device(params, chunks)

    li = li.reshape(-1)
    both = jnp.sum(sums, axis=1) + match_sums
    met = send(jnp.concatenate([li[512:], both]), fc=1)
    met, weights = tied(met, weights)
    li_half, both = li[:512] + met[:512], both + met[512:]
    plane = jnp.concatenate([lt.reshape(-1), both])
    plane = plane + send(plane, fy=1)
    others = jnp.dot(weights[512:], texts, preferred_element_type=f32).astype(f16)
    loss_rows = [parts_of(li_half[k * 128 - Q : k * 128 + Q]) for k in (3, 2, 1)]
    loss_rows = [two_rows(parts, width) for parts in (*loss_rows, parts_of(li_half[448:]))]
    plane, others, *loss_rows = tied(plane, others, *loss_rows)
    plane = plane + send(plane, fx=1)
    rows_met = send(others, fc=1)
    gt16 = lax.dot_general(
        weights, images, (((0,), (0,)), ((), ())), preferred_element_type=f32
    ).astype(f16)
    plane, gt16, rows_met = tied(plane, gt16, rows_met)
    plane = plane + send(plane, fy=3)
    half = jnp.dot(weights[:512], texts, preferred_element_type=f32) + rows_met.astype(f32)
    flight = half[Q:].astype(f16)
    plane, gt16, half, flight = tied(plane, gt16, half, flight)
    plane = plane + send(plane, fx=2)
    back_xy = lax.all_to_all(gt16, ("yh", "x", "yl"), 0, 0, tiled=True)
    text_loss = lax.dynamic_slice_in_dim(plane, ((yh * 4 + x) * 2 + yl) * Q, Q, 0)
    place = (lax.broadcasted_iota(jnp.int32, (NZ, 2), 0) == z).astype(f32)
    here = parts_of((place * plane[None, 1024:]).reshape(-1) * SUM_SCALE)
    sum_rows = two_rows(here, width)
    far = send(jnp.concatenate([flight[384:], extra_rows(loss_rows[3], sum_rows)]), dz=4)
    three, two, one = (
        send(
            jnp.concatenate(
                [
                    flight[(k - 1) * 128 : k * 128],
                    extra_rows(loss_rows[3 - k], sum_rows),
                ]
            ),
            split_z=k,
        )
        for k in (3, 2, 1)
    )
    far, three, two, one = tied(far, three, two, one)
    arrived = one.astype(f32) + two.astype(f32) + three.astype(f32)
    theirs = jnp.concatenate([lax.dynamic_slice_in_dim(arrived, (1 - core) * Q, Q, 0), arrived[128:]])
    met = send(theirs, fc=1)
    gt_own = jnp.sum(back_xy.reshape(16, Q, -1).astype(f32), axis=0)
    here_row = jnp.pad(jnp.stack(here), ((0, 0), (0, 128 - 2 * NZ)))
    grad_image, grad_text, image_loss, both = finish(
        half[:Q], far.astype(f32), arrived, met, gt_own, image_unit, text_unit, image_inv, text_inv,
        match_weight[:, None], (li_half[:Q] + match_loss)[None], here_row,
    )
    image_loss, both, text_loss = image_loss.reshape(Q), both.reshape(2), text_loss + match_loss
    return (grad_image, grad_text, image_loss, text_loss, both)


def solution(mesh):
    fine = Mesh(mesh.devices.reshape(YH, NZ, NX, YL, NC), AXES)
    dp = ("yh", "z", "x")
    in_specs = (P(dp, None), P(dp, None), P(), P())
    out_specs = (P(AXES, None), P(AXES, None), P(AXES), P(AXES), P())
    return jax.shard_map(
        per_device, mesh=fine, in_specs=in_specs, out_specs=out_specs, check_vma=False
    )
```

```python
import jax
import jax.numpy as jnp
from jax import lax
from jax.experimental import pallas as pl
from jax.experimental.pallas import tpu as pltpu
from jax.sharding import Mesh, PartitionSpec as P

AXES = ("yh", "z", "x", "yl", "core")
YH, NZ, NX, YL, NC = 2, 8, 4, 2, 2
Q = 64


def table(move):
    pairs = []
    for yh in range(YH):
        for z in range(NZ):
            for x in range(NX):
                for yl in range(YL):
                    for c in range(NC):
                        y2, z2, x2, c2 = move(yh * 2 + yl, z, x, c)
                        y2, z2, x2 = y2 % 4, z2 % NZ, x2 % NX
                        source = (((yh * NZ + z) * NX + x) * YL + yl) * NC + c
                        target = (((y2 // 2 * NZ + z2) * NX + x2) * YL + y2 % 2) * NC + c2
                        pairs.append((source, target))
    return pairs


def send(value, dx=0, dz=0, fy=0, fz=0, fx=0, fc=0, split_z=0):
    pairs = table(
        lambda y, z, x, c: (y ^ fy, (z + dz + (1 - 2 * c) * split_z) ^ fz, (x + dx) ^ fx, c ^ fc)
    )
    return lax.ppermute(value, AXES, pairs)


def rounded(value):
    return lax.reduce_precision(value, 8, 7)


def parts_of(values):
    high = lax.reduce_precision(values, 5, 10)
    return high, lax.reduce_precision(values - high, 5, 10)


def extra_rows(parts, width):
    rows = jnp.stack(parts)
    return jnp.pad(rows, ((0, 6), (0, width - rows.shape[1]))).astype(jnp.float16)


def normalize(embedding):
    floats = embedding.astype(jnp.float32)
    inverse = lax.rsqrt(jnp.sum(floats * floats, axis=-1, keepdims=True) + 1e-06)
    return (floats * inverse, inverse)


ROWS = 256


def pair_kernel(par_ref, *refs):
    a0, r1, r2, r3, r4, met = refs[:6]
    txt_in = refs[6:14]
    w_out, img_out, txt_out, li_ref, lt_ref, sums_ref, w_ref, img, txt, sems = refs[14:]
    x, yh, core = lax.axis_index("x"), lax.axis_index("yh"), lax.axis_index("core")
    img[0:64, :] = a0[pl.ds(pl.multiple_of(core * Q, Q), Q), :]
    img[64:448, :] = met[0:384, :]
    img[448:512, :] = r4[...]
    img[512:576, :] = a0[pl.ds(pl.multiple_of((1 - core) * Q, Q), Q), :]
    img[576:704, :] = r1[...]
    img[704:832, :] = r2[...]
    img[832:960, :] = r3[...]
    img[960:1024, :] = met[384:448, :]
    text_places = [
        (h * NX + lax.rem(x + dx, NX)) * 2 for h in (yh, 1 - yh) for dx in (0, NX - 1, 1, 2)
    ]
    own_column = (text_places[0] + lax.axis_index("yl")) * Q
    for k, ref in enumerate(txt_in):
        rows = ref.shape[0]
        txt[pl.ds(pl.multiple_of(text_places[k] * Q, Q), rows), :] = ref[...]
    copies = [pltpu.make_async_copy(txt, txt_out, sems.at[0]), pltpu.make_async_copy(img, img_out, sems.at[1])]
    for copy in copies:
        copy.start()
    temperature = par_ref[0]
    offset = par_ref[1]
    texts = txt[...]
    loss_cols = slope_sum = scale_sum = None
    for r in range(1024 // ROWS):
        images = img[r * ROWS : (r + 1) * ROWS, :]
        scores = lax.dot_general(
            images, texts, (((1,), (1,)), ((), ())), preferred_element_type=jnp.float32
        )
        p = jnp.exp(scores * temperature + offset)
        if r == 0:
            row = lax.broadcasted_iota(jnp.int32, (ROWS, 1024), 0)
            column = lax.broadcasted_iota(jnp.int32, (ROWS, 1024), 1)
            match = (column - row == own_column) & (row < Q)
            p = jnp.where(match, 0.0, p)
        q = 1.0 + p
        slopes = p / q
        losses = jnp.where(p < 0.0009765625, p - 0.5 * p * p, jnp.log(q))
        weights = (temperature * slopes).astype(jnp.bfloat16)
        band = pl.ds(r * ROWS, ROWS)
        w_ref[band, :] = weights
        copy = pltpu.make_async_copy(w_ref.at[band], w_out.at[band], sems.at[2 + r])
        copy.start()
        copies.append(copy)
        li_ref[r * ROWS : (r + 1) * ROWS, :] = jnp.sum(losses, axis=1, keepdims=True)
        cols = jnp.sum(losses, axis=0, keepdims=True)
        s1 = jnp.sum(slopes, axis=0, keepdims=True)
        s2 = jnp.sum(slopes * scores, axis=0, keepdims=True)
        if r == 0:
            loss_cols, slope_sum, scale_sum = cols, s1, s2
        else:
            loss_cols, slope_sum, scale_sum = loss_cols + cols, slope_sum + s1, scale_sum + s2
    lt_ref[...] = loss_cols
    sums_ref[0:1, :] = temperature * scale_sum
    sums_ref[1:2, :] = slope_sum
    for copy in copies:
        copy.wait()


def pairs_on_device(params, chunks):
    width = chunks[0].shape[1]
    vmem = pl.BlockSpec(memory_space=pltpu.VMEM)
    smem = pl.BlockSpec(memory_space=pltpu.SMEM)
    f32 = jnp.float32
    return pl.pallas_call(
        pair_kernel,
        out_shape=(
            pltpu.HBM((1024, 1024), jnp.bfloat16),
            pltpu.HBM((1024, width), jnp.bfloat16),
            pltpu.HBM((1024, width), jnp.bfloat16),
            jax.ShapeDtypeStruct((1024, 1), f32),
            jax.ShapeDtypeStruct((1, 1024), f32),
            jax.ShapeDtypeStruct((2, 1024), f32),
        ),
        in_specs=[smem] + [vmem] * len(chunks),
        out_specs=(pl.BlockSpec(memory_space=pltpu.HBM),) * 3 + (vmem,) * 3,
        scratch_shapes=[
            pltpu.VMEM((1024, 1024), jnp.bfloat16),
            pltpu.VMEM((1024, width), jnp.bfloat16),
            pltpu.VMEM((1024, width), jnp.bfloat16),
            pltpu.SemaphoreType.DMA((6,)),
        ],
        compiler_params=pltpu.CompilerParams(vmem_limit_bytes=28 * 1024 * 1024),
        cost_estimate=pl.CostEstimate(
            flops=2 * 1024 * 1024 * width, bytes_accessed=12 * 1024 * 1024, transcendentals=3 * 1024 * 1024
        ),
        name="pairs",
    )(params, *chunks)


def finish_kernel(
    half, far, arrived, met, gt, image_unit, text_unit, image_inv, text_inv, weight, loss, gi_out, gt_out, loss_out
):
    core = lax.axis_index("core")
    own = arrived[pl.ds(pl.multiple_of(core * Q, Q), Q), :]
    gi = half[...] + far[0:Q, :] + own + met[0:Q, :]
    images, texts, w = image_unit[...], text_unit[...], weight[...]
    gi = gi + w * texts.astype(jnp.bfloat16).astype(jnp.float32)
    gi_out[...] = image_inv[...] * (gi - images * jnp.sum(images * gi, axis=-1, keepdims=True))
    gt = gt[...] + w * images.astype(jnp.bfloat16).astype(jnp.float32)
    gt_out[...] = text_inv[...] * (gt - texts * jnp.sum(texts * gt, axis=-1, keepdims=True))
    near = arrived[128:130, 0:128] + met[Q : Q + 2, 0:128]
    near = jnp.where(core == 0, near[:, :Q], near[:, Q:]) + far[Q : Q + 2, 0:Q]
    loss_out[...] = loss[...] + near[0:1] + near[1:2]


def finish(*args):
    width = args[0].shape[1]
    shape = jax.ShapeDtypeStruct((Q, width), jnp.float32)
    return pl.pallas_call(
        finish_kernel,
        out_shape=(
            shape,
            shape,
            jax.ShapeDtypeStruct((1, Q), jnp.float32),
        ),
        compiler_params=pltpu.CompilerParams(vmem_limit_bytes=12 * 1024 * 1024),
        name="finish",
    )(*args)


def tied(*values):
    return lax.optimization_barrier(values)


def gather(a0, t0, core, own):
    r1 = send(a0, split_z=1)
    r4 = send(lax.dynamic_slice_in_dim(a0, core * Q, Q, 0), dz=4)
    xm, xp, c0 = send(t0, dx=1), send(t0, dx=-1), send(t0, fy=3)
    r1, t0, xm, xp, c0 = tied(r1, t0, xm, xp, c0)
    r3, r2 = send(r1, split_z=2), send(r1, split_z=1)
    cm, cp = send(c0, dx=1), send(c0, dx=-1)
    f1, f2 = send(xm[:Q], dx=1), send(xp[Q:], dx=-1)
    r2, r3, r4, cm, cp, f1, f2, *own = tied(r2, r3, r4, cm, cp, f1, f2, *own)
    g1, g2 = send(cm[:Q], dx=1), send(cp[Q:], dx=-1)
    met = send(jnp.concatenate([r1, r2, r3, r4], axis=0), fc=1)
    far = jnp.concatenate([f1, f2], axis=0)
    far_h = jnp.concatenate([g1, g2], axis=0)
    return [a0, r1, r2, r3, r4, met, t0, xm, xp, far, c0, cm, cp, far_h], own


def per_device(image_raw, text_raw, logit_scale_logarithm, logit_offset_bias):
    z, x = lax.axis_index("z"), lax.axis_index("x")
    width = image_raw.shape[1]
    yh, yl, core = lax.axis_index("yh"), lax.axis_index("yl"), lax.axis_index("core")
    f32, f16, bf16 = jnp.float32, jnp.float16, jnp.bfloat16

    def quarter(block, l, c):
        return lax.dynamic_slice_in_dim(block, (l * 2 + c) * Q, Q, 0)

    a0 = normalize(lax.dynamic_slice_in_dim(image_raw, yl * 2 * Q, 2 * Q, 0))[0].astype(bf16)
    t0 = jnp.concatenate([quarter(text_raw, 0, core), quarter(text_raw, 1, core)], axis=0)
    t0 = normalize(t0)[0].astype(bf16)
    image_unit, image_inv = normalize(quarter(image_raw, yl, core))
    text_unit, text_inv = normalize(quarter(text_raw, yl, core))
    temperature, offset = jnp.exp(logit_scale_logarithm[0]), logit_offset_bias[0]
    params = jnp.stack([temperature, offset])

    image_low, text_low = rounded(image_unit), rounded(text_unit)
    match = jnp.sum(image_low * text_low, axis=-1)
    match_logit = temperature * match + offset
    match_loss = jnp.log1p(jnp.exp(-match_logit))
    match_slope = -1.0 / (1.0 + jnp.exp(match_logit))
    match_weight = rounded(temperature * match_slope)
    match_sums = jnp.stack([temperature * jnp.sum(match_slope * match), jnp.sum(match_slope)])
    own = (image_unit, text_unit, image_inv, text_inv, match_loss, match_weight, match_sums)
    chunks, own = gather(a0, t0, core, own)
    image_unit, text_unit, image_inv, text_inv, match_loss, match_weight, match_sums = own
    weights, images, texts, li, lt, sums = pairs_on_device(params, chunks)

    li = li.reshape(-1)
    both = jnp.sum(sums, axis=1) + match_sums
    met = send(jnp.concatenate([li[512:], both]), fc=1)
    met, weights = tied(met, weights)
    li_half, both = li[:512] + met[:512], both + met[512:]
    both = both + send(both, fz=1)
    others = jnp.dot(weights[512:], texts, preferred_element_type=f32).astype(f16)
    loss_rows = [parts_of(li_half[k * 128 - Q : k * 128 + Q]) for k in (1, 2, 3)]
    loss_rows = [extra_rows(parts, width) for parts in (*loss_rows, parts_of(li_half[448:]))]
    both, others, *loss_rows = tied(both, others, *loss_rows)
    both = both + send(both, fz=2)
    rows_met = send(others, fc=1)
    gt16 = lax.dot_general(
        weights, images, (((0,), (0,)), ((), ())), preferred_element_type=f32
    ).astype(f16)
    both, gt16, rows_met = tied(both, gt16, rows_met)
    back_xy = lax.all_to_all(gt16, ("yh", "x", "yl"), 0, 0, tiled=True)
    both = both + send(both, fz=4)
    half = jnp.dot(weights[:512], texts, preferred_element_type=f32) + rows_met.astype(f32)
    flight = half[Q:].astype(f16)
    both, half, flight = tied(both, half, flight)
    far = send(jnp.concatenate([flight[384:], loss_rows[3]]), dz=4)
    three, two, one = (
        send(jnp.concatenate([flight[(k - 1) * 128 : k * 128], loss_rows[k - 1]]), split_z=k) for k in (3, 2, 1)
    )
    far, three, two, one = tied(far, three, two, one)
    arrived = one.astype(f32) + two.astype(f32) + three.astype(f32)
    theirs = jnp.concatenate([lax.dynamic_slice_in_dim(arrived, (1 - core) * Q, Q, 0), arrived[128:]])
    met = send(theirs, fc=1)
    gt_own = jnp.sum(back_xy.reshape(16, Q, -1).astype(f32), axis=0)
    grad_image, grad_text, image_loss = finish(
        half[:Q], far.astype(f32), arrived, met, gt_own, image_unit, text_unit, image_inv, text_inv,
        match_weight[:, None], (li_half[:Q] + match_loss)[None],
    )
    lt, both, _ = tied(lt, both, back_xy)
    plane = jnp.concatenate([lt.reshape(-1), both])
    for move in (dict(fy=1), dict(fx=1), dict(fy=3), dict(fx=2)):
        plane = plane + send(plane, **move)
    text_loss = lax.dynamic_slice_in_dim(plane, ((yh * 4 + x) * 2 + yl) * Q, Q, 0) + match_loss
    image_loss, both = image_loss.reshape(Q), plane[1024:]
    return (grad_image, grad_text, image_loss, text_loss, both)


def solution(mesh):
    fine = Mesh(mesh.devices.reshape(YH, NZ, NX, YL, NC), AXES)
    dp = ("yh", "z", "x")
    in_specs = (P(dp, None), P(dp, None), P(), P())
    out_specs = (P(AXES, None), P(AXES, None), P(AXES), P(AXES), P())
    return jax.shard_map(
        per_device, mesh=fine, in_specs=in_specs, out_specs=out_specs, check_vma=False
    )
```

```python
import jax
import jax.numpy as jnp
from jax import lax
from jax.experimental import pallas as pl
from jax.experimental.pallas import tpu as pltpu
from jax.sharding import Mesh, PartitionSpec as P

AXES = ("yh", "z", "x", "yl", "core")
YH, NZ, NX, YL, NC = 2, 8, 4, 2, 2
Q = 64


def table(move):
    pairs = []
    for yh in range(YH):
        for z in range(NZ):
            for x in range(NX):
                for yl in range(YL):
                    for c in range(NC):
                        y2, z2, x2, c2 = move(yh * 2 + yl, z, x, c)
                        y2, z2, x2 = y2 % 4, z2 % NZ, x2 % NX
                        source = (((yh * NZ + z) * NX + x) * YL + yl) * NC + c
                        target = (((y2 // 2 * NZ + z2) * NX + x2) * YL + y2 % 2) * NC + c2
                        pairs.append((source, target))
    return pairs


def send(value, dx=0, dz=0, fy=0, fz=0, fx=0, fc=0, split_z=0):
    pairs = table(
        lambda y, z, x, c: (y ^ fy, (z + dz + (1 - 2 * c) * split_z) ^ fz, (x + dx) ^ fx, c ^ fc)
    )
    return lax.ppermute(value, AXES, pairs)


def rounded(value):
    return lax.reduce_precision(value, 8, 7)


def parts_of(values):
    high = lax.reduce_precision(values, 5, 10)
    return high, lax.reduce_precision(values - high, 5, 10)


def extra_rows(parts, width):
    rows = jnp.stack(parts)
    return jnp.pad(rows, ((0, 6), (0, width - rows.shape[1]))).astype(jnp.float16)


def normalize(embedding):
    floats = embedding.astype(jnp.float32)
    inverse = lax.rsqrt(jnp.sum(floats * floats, axis=-1, keepdims=True) + 1e-06)
    return (floats * inverse, inverse)


ROWS = 256


def pair_kernel(par_ref, *refs):
    a0, r1, r2, r3, r4, met = refs[:6]
    txt_in = refs[6:14]
    w_out, img_out, txt_out, li_ref, lt_ref, sums_ref, w_ref, img, txt, sems = refs[14:]
    x, yh, core = lax.axis_index("x"), lax.axis_index("yh"), lax.axis_index("core")
    img[0:64, :] = a0[pl.ds(pl.multiple_of(core * Q, Q), Q), :]
    img[64:448, :] = met[0:384, :]
    img[448:512, :] = r4[...]
    img[512:576, :] = a0[pl.ds(pl.multiple_of((1 - core) * Q, Q), Q), :]
    img[576:704, :] = r1[...]
    img[704:832, :] = r2[...]
    img[832:960, :] = r3[...]
    img[960:1024, :] = met[384:448, :]
    text_places = [
        (h * NX + lax.rem(x + dx, NX)) * 2 for h in (yh, 1 - yh) for dx in (0, NX - 1, 1, 2)
    ]
    own_column = (text_places[0] + lax.axis_index("yl")) * Q
    for k, ref in enumerate(txt_in):
        rows = ref.shape[0]
        txt[pl.ds(pl.multiple_of(text_places[k] * Q, Q), rows), :] = ref[...]
    copies = [pltpu.make_async_copy(txt, txt_out, sems.at[0]), pltpu.make_async_copy(img, img_out, sems.at[1])]
    for copy in copies:
        copy.start()
    temperature = par_ref[0]
    offset = par_ref[1]
    texts = txt[...]
    loss_cols = slope_sum = scale_sum = None
    for r in range(1024 // ROWS):
        images = img[r * ROWS : (r + 1) * ROWS, :]
        scores = lax.dot_general(
            images, texts, (((1,), (1,)), ((), ())), preferred_element_type=jnp.float32
        )
        p = jnp.exp(scores * temperature + offset)
        if r == 0:
            row = lax.broadcasted_iota(jnp.int32, (ROWS, 1024), 0)
            column = lax.broadcasted_iota(jnp.int32, (ROWS, 1024), 1)
            match = (column - row == own_column) & (row < Q)
            p = jnp.where(match, 0.0, p)
        q = 1.0 + p
        slopes = p / q
        losses = jnp.where(p < 0.0009765625, p - 0.5 * p * p, jnp.log(q))
        weights = (temperature * slopes).astype(jnp.bfloat16)
        band = pl.ds(r * ROWS, ROWS)
        w_ref[band, :] = weights
        copy = pltpu.make_async_copy(w_ref.at[band], w_out.at[band], sems.at[2 + r])
        copy.start()
        copies.append(copy)
        li_ref[r * ROWS : (r + 1) * ROWS, :] = jnp.sum(losses, axis=1, keepdims=True)
        cols = jnp.sum(losses, axis=0, keepdims=True)
        s1 = jnp.sum(slopes, axis=0, keepdims=True)
        s2 = jnp.sum(slopes * scores, axis=0, keepdims=True)
        if r == 0:
            loss_cols, slope_sum, scale_sum = cols, s1, s2
        else:
            loss_cols, slope_sum, scale_sum = loss_cols + cols, slope_sum + s1, scale_sum + s2
    lt_ref[...] = loss_cols
    sums_ref[0:1, :] = temperature * scale_sum
    sums_ref[1:2, :] = slope_sum
    for copy in copies:
        copy.wait()


def pairs_on_device(params, chunks):
    width = chunks[0].shape[1]
    vmem = pl.BlockSpec(memory_space=pltpu.VMEM)
    smem = pl.BlockSpec(memory_space=pltpu.SMEM)
    f32 = jnp.float32
    return pl.pallas_call(
        pair_kernel,
        out_shape=(
            pltpu.HBM((1024, 1024), jnp.bfloat16),
            pltpu.HBM((1024, width), jnp.bfloat16),
            pltpu.HBM((1024, width), jnp.bfloat16),
            jax.ShapeDtypeStruct((1024, 1), f32),
            jax.ShapeDtypeStruct((1, 1024), f32),
            jax.ShapeDtypeStruct((2, 1024), f32),
        ),
        in_specs=[smem] + [vmem] * len(chunks),
        out_specs=(pl.BlockSpec(memory_space=pltpu.HBM),) * 3 + (vmem,) * 3,
        scratch_shapes=[
            pltpu.VMEM((1024, 1024), jnp.bfloat16),
            pltpu.VMEM((1024, width), jnp.bfloat16),
            pltpu.VMEM((1024, width), jnp.bfloat16),
            pltpu.SemaphoreType.DMA((6,)),
        ],
        compiler_params=pltpu.CompilerParams(vmem_limit_bytes=28 * 1024 * 1024),
        cost_estimate=pl.CostEstimate(
            flops=2 * 1024 * 1024 * width, bytes_accessed=12 * 1024 * 1024, transcendentals=3 * 1024 * 1024
        ),
        name="pairs",
    )(params, *chunks)


def finish_kernel(
    half, far, arrived, met, gt, image_unit, text_unit, image_inv, text_inv, weight, loss, gi_out, gt_out, loss_out
):
    core = lax.axis_index("core")
    own = arrived[pl.ds(pl.multiple_of(core * Q, Q), Q), :]
    gi = half[...] + far[0:Q, :] + own + met[0:Q, :]
    images, texts, w = image_unit[...], text_unit[...], weight[...]
    gi = gi + w * texts.astype(jnp.bfloat16).astype(jnp.float32)
    gi_out[...] = image_inv[...] * (gi - images * jnp.sum(images * gi, axis=-1, keepdims=True))
    gt = gt[...] + w * images.astype(jnp.bfloat16).astype(jnp.float32)
    gt_out[...] = text_inv[...] * (gt - texts * jnp.sum(texts * gt, axis=-1, keepdims=True))
    near = arrived[128:130, 0:128] + met[Q : Q + 2, 0:128]
    near = jnp.where(core == 0, near[:, :Q], near[:, Q:]) + far[Q : Q + 2, 0:Q]
    loss_out[...] = loss[...] + near[0:1] + near[1:2]


def finish(*args):
    width = args[0].shape[1]
    shape = jax.ShapeDtypeStruct((Q, width), jnp.float32)
    return pl.pallas_call(
        finish_kernel,
        out_shape=(
            shape,
            shape,
            jax.ShapeDtypeStruct((1, Q), jnp.float32),
        ),
        compiler_params=pltpu.CompilerParams(vmem_limit_bytes=12 * 1024 * 1024),
        name="finish",
    )(*args)


def tied(*values):
    return lax.optimization_barrier(values)


def gather(a0, t0, core, own):
    r1 = send(a0, split_z=1)
    r4 = send(lax.dynamic_slice_in_dim(a0, core * Q, Q, 0), dz=4)
    xm, xp, c0 = send(t0, dx=1), send(t0, dx=-1), send(t0, fy=3)
    r1, t0, xm, xp, c0 = tied(r1, t0, xm, xp, c0)
    r3, r2 = send(r1, split_z=2), send(r1, split_z=1)
    cm, cp = send(c0, dx=1), send(c0, dx=-1)
    f1, f2 = send(xm[:Q], dx=1), send(xp[Q:], dx=-1)
    r2, r3, r4, cm, cp, f1, f2, *own = tied(r2, r3, r4, cm, cp, f1, f2, *own)
    g1, g2 = send(cm[:Q], dx=1), send(cp[Q:], dx=-1)
    met = send(jnp.concatenate([r1, r2, r3, r4], axis=0), fc=1)
    far = jnp.concatenate([f1, f2], axis=0)
    far_h = jnp.concatenate([g1, g2], axis=0)
    return [a0, r1, r2, r3, r4, met, t0, xm, xp, far, c0, cm, cp, far_h], own


def per_device(image_raw, text_raw, logit_scale_logarithm, logit_offset_bias):
    z, x = lax.axis_index("z"), lax.axis_index("x")
    width = image_raw.shape[1]
    yh, yl, core = lax.axis_index("yh"), lax.axis_index("yl"), lax.axis_index("core")
    f32, f16, bf16 = jnp.float32, jnp.float16, jnp.bfloat16

    def quarter(block, l, c):
        return lax.dynamic_slice_in_dim(block, (l * 2 + c) * Q, Q, 0)

    a0 = normalize(lax.dynamic_slice_in_dim(image_raw, yl * 2 * Q, 2 * Q, 0))[0].astype(bf16)
    t0 = jnp.concatenate([quarter(text_raw, 0, core), quarter(text_raw, 1, core)], axis=0)
    t0 = normalize(t0)[0].astype(bf16)
    image_unit, image_inv = normalize(quarter(image_raw, yl, core))
    text_unit, text_inv = normalize(quarter(text_raw, yl, core))
    temperature, offset = jnp.exp(logit_scale_logarithm[0]), logit_offset_bias[0]
    params = jnp.stack([temperature, offset])

    image_low, text_low = rounded(image_unit), rounded(text_unit)
    match = jnp.sum(image_low * text_low, axis=-1)
    match_logit = temperature * match + offset
    match_loss = jnp.log1p(jnp.exp(-match_logit))
    match_slope = -1.0 / (1.0 + jnp.exp(match_logit))
    match_weight = rounded(temperature * match_slope)
    match_sums = jnp.stack([temperature * jnp.sum(match_slope * match), jnp.sum(match_slope)])
    own = (image_unit, text_unit, image_inv, text_inv, match_loss, match_weight, match_sums)
    chunks, own = gather(a0, t0, core, own)
    image_unit, text_unit, image_inv, text_inv, match_loss, match_weight, match_sums = own
    weights, images, texts, li, lt, sums = pairs_on_device(params, chunks)

    li = li.reshape(-1)
    both = jnp.sum(sums, axis=1) + match_sums
    met = send(jnp.concatenate([li[512:], both]), fc=1)
    met, weights = tied(met, weights)
    li_half, both = li[:512] + met[:512], both + met[512:]
    both = both + send(both, fz=1)
    others = jnp.dot(weights[512:], texts, preferred_element_type=f32).astype(f16)
    loss_rows = [parts_of(li_half[k * 128 - Q : k * 128 + Q]) for k in (1, 2, 3)]
    loss_rows = [extra_rows(parts, width) for parts in (*loss_rows, parts_of(li_half[448:]))]
    both, others, *loss_rows = tied(both, others, *loss_rows)
    both = both + send(both, fz=2)
    rows_met = send(others, fc=1)
    gt16 = lax.dot_general(
        weights, images, (((0,), (0,)), ((), ())), preferred_element_type=f32
    ).astype(f16)
    both, gt16, rows_met = tied(both, gt16, rows_met)
    back_xy = lax.all_to_all(gt16, ("yh", "x", "yl"), 0, 0, tiled=True)
    both = both + send(both, fz=4)
    half = jnp.dot(weights[:512], texts, preferred_element_type=f32) + rows_met.astype(f32)
    flight = half[Q:].astype(f16)
    both, half, flight = tied(both, half[:Q], flight)
    far = send(jnp.concatenate([flight[384:], loss_rows[3]]), dz=4)
    three, two, one = (
        send(jnp.concatenate([flight[(k - 1) * 128 : k * 128], loss_rows[k - 1]]), split_z=k) for k in (3, 2, 1)
    )
    plane = jnp.concatenate([lt.reshape(-1), both])
    plane = plane + send(plane, fy=1)
    plane, far, three = tied(plane, far, three)
    for move in (dict(fx=1), dict(fy=3)):
        plane = plane + send(plane, **move)
    arrived = one.astype(f32) + two.astype(f32) + three.astype(f32)
    theirs = jnp.concatenate([lax.dynamic_slice_in_dim(arrived, (1 - core) * Q, Q, 0), arrived[128:]])
    plane, far, arrived, theirs = tied(plane, far, arrived, theirs)
    met = send(theirs, fc=1)
    plane = plane + send(plane, fx=2)
    gt_own = jnp.sum(back_xy.reshape(16, Q, -1).astype(f32), axis=0)
    grad_image, grad_text, image_loss = finish(
        half, far.astype(f32), arrived, met, gt_own, image_unit, text_unit, image_inv, text_inv,
        match_weight[:, None], (li_half[:Q] + match_loss)[None],
    )
    text_loss = lax.dynamic_slice_in_dim(plane, ((yh * 4 + x) * 2 + yl) * Q, Q, 0) + match_loss
    image_loss, both = image_loss.reshape(Q), plane[1024:]
    return (grad_image, grad_text, image_loss, text_loss, both)


def solution(mesh):
    fine = Mesh(mesh.devices.reshape(YH, NZ, NX, YL, NC), AXES)
    dp = ("yh", "z", "x")
    in_specs = (P(dp, None), P(dp, None), P(), P())
    out_specs = (P(AXES, None), P(AXES, None), P(AXES), P(AXES), P())
    return jax.shard_map(
        per_device, mesh=fine, in_specs=in_specs, out_specs=out_specs, check_vma=False
    )
```

```python
import jax
import jax.numpy as jnp
from jax import lax
from jax.experimental import pallas as pl
from jax.experimental.pallas import tpu as pltpu
from jax.sharding import Mesh, PartitionSpec as P

AXES = ("yh", "z", "x", "yl", "core")
YH, NZ, NX, YL, NC = 2, 8, 4, 2, 2
Q = 64


def table(move):
    pairs = []
    for yh in range(YH):
        for z in range(NZ):
            for x in range(NX):
                for yl in range(YL):
                    for c in range(NC):
                        y2, z2, x2, c2 = move(yh * 2 + yl, z, x, c)
                        y2, z2, x2 = y2 % 4, z2 % NZ, x2 % NX
                        source = (((yh * NZ + z) * NX + x) * YL + yl) * NC + c
                        target = (((y2 // 2 * NZ + z2) * NX + x2) * YL + y2 % 2) * NC + c2
                        pairs.append((source, target))
    return pairs


def send(value, dx=0, dz=0, fy=0, fz=0, fx=0, fc=0, split_z=0):
    pairs = table(
        lambda y, z, x, c: (y ^ fy, (z + dz + (1 - 2 * c) * split_z) ^ fz, (x + dx) ^ fx, c ^ fc)
    )
    return lax.ppermute(value, AXES, pairs)


def rounded(value):
    return lax.reduce_precision(value, 8, 7)


def parts_of(values):
    high = lax.reduce_precision(values, 5, 10)
    return high, lax.reduce_precision(values - high, 5, 10)


def extra_rows(parts, width):
    rows = jnp.stack(parts)
    return jnp.pad(rows, ((0, 6), (0, width - rows.shape[1]))).astype(jnp.float16)


def normalize(embedding):
    floats = embedding.astype(jnp.float32)
    inverse = lax.rsqrt(jnp.sum(floats * floats, axis=-1, keepdims=True) + 1e-06)
    return (floats * inverse, inverse)


ROWS = 256


def pair_kernel(par_ref, *refs):
    a0, r1, r2, r3, r4, met = refs[:6]
    txt_in = refs[6:14]
    w_out, img_out, txt_out, li_ref, lt_ref, sums_ref, w_ref, img, txt, sems = refs[14:]
    x, yh, core = lax.axis_index("x"), lax.axis_index("yh"), lax.axis_index("core")
    img[0:64, :] = a0[pl.ds(pl.multiple_of(core * Q, Q), Q), :]
    img[64:448, :] = met[0:384, :]
    img[448:512, :] = r4[...]
    img[512:576, :] = a0[pl.ds(pl.multiple_of((1 - core) * Q, Q), Q), :]
    img[576:704, :] = r1[...]
    img[704:832, :] = r2[...]
    img[832:960, :] = r3[...]
    img[960:1024, :] = met[384:448, :]
    text_places = [
        (h * NX + lax.rem(x + dx, NX)) * 2 for h in (yh, 1 - yh) for dx in (0, NX - 1, 1, 2)
    ]
    own_column = (text_places[0] + lax.axis_index("yl")) * Q
    for k, ref in enumerate(txt_in):
        rows = ref.shape[0]
        txt[pl.ds(pl.multiple_of(text_places[k] * Q, Q), rows), :] = ref[...]
    copies = [pltpu.make_async_copy(txt, txt_out, sems.at[0]), pltpu.make_async_copy(img, img_out, sems.at[1])]
    for copy in copies:
        copy.start()
    temperature = par_ref[0]
    offset = par_ref[1]
    texts = txt[...]
    loss_cols = slope_sum = scale_sum = None
    for r in range(1024 // ROWS):
        images = img[r * ROWS : (r + 1) * ROWS, :]
        scores = lax.dot_general(
            images, texts, (((1,), (1,)), ((), ())), preferred_element_type=jnp.float32
        )
        p = jnp.exp(scores * temperature + offset)
        if r == 0:
            row = lax.broadcasted_iota(jnp.int32, (ROWS, 1024), 0)
            column = lax.broadcasted_iota(jnp.int32, (ROWS, 1024), 1)
            match = (column - row == own_column) & (row < Q)
            p = jnp.where(match, 0.0, p)
        q = 1.0 + p
        slopes = p / q
        losses = jnp.where(p < 0.0009765625, p - 0.5 * p * p, jnp.log(q))
        weights = (temperature * slopes).astype(jnp.bfloat16)
        band = pl.ds(r * ROWS, ROWS)
        w_ref[band, :] = weights
        copy = pltpu.make_async_copy(w_ref.at[band], w_out.at[band], sems.at[2 + r])
        copy.start()
        copies.append(copy)
        li_ref[r * ROWS : (r + 1) * ROWS, :] = jnp.sum(losses, axis=1, keepdims=True)
        cols = jnp.sum(losses, axis=0, keepdims=True)
        s1 = jnp.sum(slopes, axis=0, keepdims=True)
        s2 = jnp.sum(slopes * scores, axis=0, keepdims=True)
        if r == 0:
            loss_cols, slope_sum, scale_sum = cols, s1, s2
        else:
            loss_cols, slope_sum, scale_sum = loss_cols + cols, slope_sum + s1, scale_sum + s2
    lt_ref[...] = loss_cols
    sums_ref[0:1, :] = temperature * scale_sum
    sums_ref[1:2, :] = slope_sum
    for copy in copies:
        copy.wait()


def pairs_on_device(params, chunks):
    width = chunks[0].shape[1]
    vmem = pl.BlockSpec(memory_space=pltpu.VMEM)
    smem = pl.BlockSpec(memory_space=pltpu.SMEM)
    f32 = jnp.float32
    return pl.pallas_call(
        pair_kernel,
        out_shape=(
            pltpu.HBM((1024, 1024), jnp.bfloat16),
            pltpu.HBM((1024, width), jnp.bfloat16),
            pltpu.HBM((1024, width), jnp.bfloat16),
            jax.ShapeDtypeStruct((1024, 1), f32),
            jax.ShapeDtypeStruct((1, 1024), f32),
            jax.ShapeDtypeStruct((2, 1024), f32),
        ),
        in_specs=[smem] + [vmem] * len(chunks),
        out_specs=(pl.BlockSpec(memory_space=pltpu.HBM),) * 3 + (vmem,) * 3,
        scratch_shapes=[
            pltpu.VMEM((1024, 1024), jnp.bfloat16),
            pltpu.VMEM((1024, width), jnp.bfloat16),
            pltpu.VMEM((1024, width), jnp.bfloat16),
            pltpu.SemaphoreType.DMA((6,)),
        ],
        compiler_params=pltpu.CompilerParams(vmem_limit_bytes=28 * 1024 * 1024),
        cost_estimate=pl.CostEstimate(
            flops=2 * 1024 * 1024 * width, bytes_accessed=12 * 1024 * 1024, transcendentals=3 * 1024 * 1024
        ),
        name="pairs",
    )(params, *chunks)


def finish_kernel(
    half, far, arrived, met, gt, image_unit, text_unit, image_inv, text_inv, weight, loss, gi_out, gt_out, loss_out
):
    core = lax.axis_index("core")
    own = arrived[pl.ds(pl.multiple_of(core * Q, Q), Q), :]
    gi = half[...] + far[0:Q, :] + own + met[0:Q, :]
    images, texts, w = image_unit[...], text_unit[...], weight[...]
    gi = gi + w * texts.astype(jnp.bfloat16).astype(jnp.float32)
    gi_out[...] = image_inv[...] * (gi - images * jnp.sum(images * gi, axis=-1, keepdims=True))
    gt = gt[...] + w * images.astype(jnp.bfloat16).astype(jnp.float32)
    gt_out[...] = text_inv[...] * (gt - texts * jnp.sum(texts * gt, axis=-1, keepdims=True))
    near = arrived[128:130, 0:128] + met[Q : Q + 2, 0:128]
    near = jnp.where(core == 0, near[:, :Q], near[:, Q:]) + far[Q : Q + 2, 0:Q]
    loss_out[...] = loss[...] + near[0:1] + near[1:2]


def finish(*args):
    width = args[0].shape[1]
    shape = jax.ShapeDtypeStruct((Q, width), jnp.float32)
    return pl.pallas_call(
        finish_kernel,
        out_shape=(
            shape,
            shape,
            jax.ShapeDtypeStruct((1, Q), jnp.float32),
        ),
        compiler_params=pltpu.CompilerParams(vmem_limit_bytes=12 * 1024 * 1024),
        name="finish",
    )(*args)


def tied(*values):
    return lax.optimization_barrier(values)


def gather(a0, t0, core, own):
    r1 = send(a0, split_z=1)
    r4 = send(lax.dynamic_slice_in_dim(a0, core * Q, Q, 0), dz=4)
    xm, xp, c0 = send(t0, dx=1), send(t0, dx=-1), send(t0, fy=3)
    r1, t0, xm, xp, c0 = tied(r1, t0, xm, xp, c0)
    r3, r2 = send(r1, split_z=2), send(r1, split_z=1)
    cm, cp = send(c0, dx=1), send(c0, dx=-1)
    f1, f2 = send(xm[:Q], dx=1), send(xp[Q:], dx=-1)
    r2, r3, r4, cm, cp, f1, f2, *own = tied(r2, r3, r4, cm, cp, f1, f2, *own)
    g1, g2 = send(cm[:Q], dx=1), send(cp[Q:], dx=-1)
    met = send(jnp.concatenate([r1, r2, r3, r4], axis=0), fc=1)
    far = jnp.concatenate([f1, f2], axis=0)
    far_h = jnp.concatenate([g1, g2], axis=0)
    return [a0, r1, r2, r3, r4, met, t0, xm, xp, far, c0, cm, cp, far_h], own


def per_device(image_raw, text_raw, logit_scale_logarithm, logit_offset_bias):
    z, x = lax.axis_index("z"), lax.axis_index("x")
    width = image_raw.shape[1]
    yh, yl, core = lax.axis_index("yh"), lax.axis_index("yl"), lax.axis_index("core")
    f32, f16, bf16 = jnp.float32, jnp.float16, jnp.bfloat16

    def quarter(block, l, c):
        return lax.dynamic_slice_in_dim(block, (l * 2 + c) * Q, Q, 0)

    a0 = normalize(lax.dynamic_slice_in_dim(image_raw, yl * 2 * Q, 2 * Q, 0))[0].astype(bf16)
    t0 = jnp.concatenate([quarter(text_raw, 0, core), quarter(text_raw, 1, core)], axis=0)
    t0 = normalize(t0)[0].astype(bf16)
    image_unit, image_inv = normalize(quarter(image_raw, yl, core))
    text_unit, text_inv = normalize(quarter(text_raw, yl, core))
    temperature, offset = jnp.exp(logit_scale_logarithm[0]), logit_offset_bias[0]
    params = jnp.stack([temperature, offset])

    image_low, text_low = rounded(image_unit), rounded(text_unit)
    match = jnp.sum(image_low * text_low, axis=-1)
    match_logit = temperature * match + offset
    match_loss = jnp.log1p(jnp.exp(-match_logit))
    match_slope = -1.0 / (1.0 + jnp.exp(match_logit))
    match_weight = rounded(temperature * match_slope)
    match_sums = jnp.stack([temperature * jnp.sum(match_slope * match), jnp.sum(match_slope)])
    own = (image_unit, text_unit, image_inv, text_inv, match_loss, match_weight, match_sums)
    chunks, own = gather(a0, t0, core, own)
    image_unit, text_unit, image_inv, text_inv, match_loss, match_weight, match_sums = own
    weights, images, texts, li, lt, sums = pairs_on_device(params, chunks)

    li = li.reshape(-1)
    both = jnp.sum(sums, axis=1) + match_sums
    met = send(jnp.concatenate([li[512:], both]), fc=1)
    met, weights = tied(met, weights)
    li_half, both = li[:512] + met[:512], both + met[512:]
    both = both + send(both, fz=1)
    others = jnp.dot(weights[512:], texts, preferred_element_type=f32).astype(f16)
    loss_rows = [parts_of(li_half[k * 128 - Q : k * 128 + Q]) for k in (1, 2, 3)]
    loss_rows = [extra_rows(parts, width) for parts in (*loss_rows, parts_of(li_half[448:]))]
    both, others, *loss_rows = tied(both, others, *loss_rows)
    both = both + send(both, fz=2)
    rows_met = send(others, fc=1)
    gt16 = lax.dot_general(
        weights, images, (((0,), (0,)), ((), ())), preferred_element_type=f32
    ).astype(f16)
    both, gt16, rows_met = tied(both, gt16, rows_met)
    back_xy = lax.all_to_all(gt16, ("yh", "x", "yl"), 0, 0, tiled=True)
    both = both + send(both, fz=4)
    half = jnp.dot(weights[:512], texts, preferred_element_type=f32) + rows_met.astype(f32)
    flight = half[Q:].astype(f16)
    both, half, flight = tied(both, half, flight)
    far = send(jnp.concatenate([flight[384:], loss_rows[3]]), dz=4)
    three, two, one = (
        send(jnp.concatenate([flight[(k - 1) * 128 : k * 128], loss_rows[k - 1]]), split_z=k) for k in (3, 2, 1)
    )
    plane = jnp.concatenate([lt.reshape(-1), both])
    for move in (dict(fy=1), dict(fx=1), dict(fy=3)):
        plane = plane + send(plane, **move)
    plane, far, three, two, one = tied(plane, far, three, two, one)
    arrived = one.astype(f32) + two.astype(f32) + three.astype(f32)
    theirs = jnp.concatenate([lax.dynamic_slice_in_dim(arrived, (1 - core) * Q, Q, 0), arrived[128:]])
    met = send(theirs, fc=1)
    plane = plane + send(plane, fx=2)
    gt_own = jnp.sum(back_xy.reshape(16, Q, -1).astype(f32), axis=0)
    grad_image, grad_text, image_loss = finish(
        half[:Q], far.astype(f32), arrived, met, gt_own, image_unit, text_unit, image_inv, text_inv,
        match_weight[:, None], (li_half[:Q] + match_loss)[None],
    )
    text_loss = lax.dynamic_slice_in_dim(plane, ((yh * 4 + x) * 2 + yl) * Q, Q, 0) + match_loss
    image_loss, both = image_loss.reshape(Q), plane[1024:]
    return (grad_image, grad_text, image_loss, text_loss, both)


def solution(mesh):
    fine = Mesh(mesh.devices.reshape(YH, NZ, NX, YL, NC), AXES)
    dp = ("yh", "z", "x")
    in_specs = (P(dp, None), P(dp, None), P(), P())
    out_specs = (P(AXES, None), P(AXES, None), P(AXES), P(AXES), P())
    return jax.shard_map(
        per_device, mesh=fine, in_specs=in_specs, out_specs=out_specs, check_vma=False
    )
```

```python
import jax
import jax.numpy as jnp
from jax import lax
from jax.experimental import pallas as pl
from jax.experimental.pallas import tpu as pltpu
from jax.sharding import Mesh, PartitionSpec as P

AXES = ("yh", "z", "x", "yl", "core")
YH, NZ, NX, YL, NC = 2, 8, 4, 2, 2
Q = 64


def table(move):
    pairs = []
    for yh in range(YH):
        for z in range(NZ):
            for x in range(NX):
                for yl in range(YL):
                    for c in range(NC):
                        y2, z2, x2, c2 = move(yh * 2 + yl, z, x, c)
                        y2, z2, x2 = y2 % 4, z2 % NZ, x2 % NX
                        source = (((yh * NZ + z) * NX + x) * YL + yl) * NC + c
                        target = (((y2 // 2 * NZ + z2) * NX + x2) * YL + y2 % 2) * NC + c2
                        pairs.append((source, target))
    return pairs


def send(value, dx=0, dz=0, fy=0, fz=0, fx=0, fc=0, split_z=0):
    pairs = table(
        lambda y, z, x, c: (y ^ fy, (z + dz + (1 - 2 * c) * split_z) ^ fz, (x + dx) ^ fx, c ^ fc)
    )
    return lax.ppermute(value, AXES, pairs)


def rounded(value):
    return lax.reduce_precision(value, 8, 7)


def parts_of(values):
    high = lax.reduce_precision(values, 5, 10)
    return high, lax.reduce_precision(values - high, 5, 10)


def extra_rows(parts, width):
    rows = jnp.stack(parts)
    return jnp.pad(rows, ((0, 6), (0, width - rows.shape[1]))).astype(jnp.float16)


def normalize(embedding):
    floats = embedding.astype(jnp.float32)
    inverse = lax.rsqrt(jnp.sum(floats * floats, axis=-1, keepdims=True) + 1e-06)
    return (floats * inverse, inverse)


ROWS = 256


def pair_kernel(par_ref, *refs):
    a0, r1, r2, r3, r4, met = refs[:6]
    txt_in = refs[6:14]
    w_out, img_out, txt_out, li_ref, lt_ref, sums_ref, w_ref, img, txt, sems = refs[14:]
    x, yh, core = lax.axis_index("x"), lax.axis_index("yh"), lax.axis_index("core")
    img[0:64, :] = a0[pl.ds(pl.multiple_of(core * Q, Q), Q), :]
    img[64:448, :] = met[0:384, :]
    img[448:512, :] = r4[...]
    img[512:576, :] = a0[pl.ds(pl.multiple_of((1 - core) * Q, Q), Q), :]
    img[576:704, :] = r1[...]
    img[704:832, :] = r2[...]
    img[832:960, :] = r3[...]
    img[960:1024, :] = met[384:448, :]
    text_places = [
        (h * NX + lax.rem(x + dx, NX)) * 2 for h in (yh, 1 - yh) for dx in (0, NX - 1, 1, 2)
    ]
    own_column = (text_places[0] + lax.axis_index("yl")) * Q
    for k, ref in enumerate(txt_in):
        rows = ref.shape[0]
        txt[pl.ds(pl.multiple_of(text_places[k] * Q, Q), rows), :] = ref[...]
    copies = [pltpu.make_async_copy(txt, txt_out, sems.at[0]), pltpu.make_async_copy(img, img_out, sems.at[1])]
    for copy in copies:
        copy.start()
    temperature = par_ref[0]
    offset = par_ref[1]
    texts = txt[...]
    loss_cols = slope_sum = scale_sum = None
    for r in range(1024 // ROWS):
        images = img[r * ROWS : (r + 1) * ROWS, :]
        scores = lax.dot_general(
            images, texts, (((1,), (1,)), ((), ())), preferred_element_type=jnp.float32
        )
        p = jnp.exp(scores * temperature + offset)
        if r == 0:
            row = lax.broadcasted_iota(jnp.int32, (ROWS, 1024), 0)
            column = lax.broadcasted_iota(jnp.int32, (ROWS, 1024), 1)
            match = (column - row == own_column) & (row < Q)
            p = jnp.where(match, 0.0, p)
        q = 1.0 + p
        slopes = p / q
        losses = jnp.where(p < 0.0009765625, p - 0.5 * p * p, jnp.log(q))
        weights = (temperature * slopes).astype(jnp.bfloat16)
        band = pl.ds(r * ROWS, ROWS)
        w_ref[band, :] = weights
        copy = pltpu.make_async_copy(w_ref.at[band], w_out.at[band], sems.at[2 + r])
        copy.start()
        copies.append(copy)
        li_ref[r * ROWS : (r + 1) * ROWS, :] = jnp.sum(losses, axis=1, keepdims=True)
        cols = jnp.sum(losses, axis=0, keepdims=True)
        s1 = jnp.sum(slopes, axis=0, keepdims=True)
        s2 = jnp.sum(slopes * scores, axis=0, keepdims=True)
        if r == 0:
            loss_cols, slope_sum, scale_sum = cols, s1, s2
        else:
            loss_cols, slope_sum, scale_sum = loss_cols + cols, slope_sum + s1, scale_sum + s2
    lt_ref[...] = loss_cols
    sums_ref[0:1, :] = temperature * scale_sum
    sums_ref[1:2, :] = slope_sum
    for copy in copies:
        copy.wait()


def pairs_on_device(params, chunks):
    width = chunks[0].shape[1]
    vmem = pl.BlockSpec(memory_space=pltpu.VMEM)
    smem = pl.BlockSpec(memory_space=pltpu.SMEM)
    f32 = jnp.float32
    return pl.pallas_call(
        pair_kernel,
        out_shape=(
            pltpu.HBM((1024, 1024), jnp.bfloat16),
            pltpu.HBM((1024, width), jnp.bfloat16),
            pltpu.HBM((1024, width), jnp.bfloat16),
            jax.ShapeDtypeStruct((1024, 1), f32),
            jax.ShapeDtypeStruct((1, 1024), f32),
            jax.ShapeDtypeStruct((2, 1024), f32),
        ),
        in_specs=[smem] + [vmem] * len(chunks),
        out_specs=(pl.BlockSpec(memory_space=pltpu.HBM),) * 3 + (vmem,) * 3,
        scratch_shapes=[
            pltpu.VMEM((1024, 1024), jnp.bfloat16),
            pltpu.VMEM((1024, width), jnp.bfloat16),
            pltpu.VMEM((1024, width), jnp.bfloat16),
            pltpu.SemaphoreType.DMA((6,)),
        ],
        compiler_params=pltpu.CompilerParams(vmem_limit_bytes=28 * 1024 * 1024),
        cost_estimate=pl.CostEstimate(
            flops=2 * 1024 * 1024 * width, bytes_accessed=12 * 1024 * 1024, transcendentals=3 * 1024 * 1024
        ),
        name="pairs",
    )(params, *chunks)


def finish_kernel(
    half, far, arrived, met, gt, image_unit, text_unit, image_inv, text_inv, weight, loss, gi_out, gt_out, loss_out
):
    core = lax.axis_index("core")
    own = arrived[pl.ds(pl.multiple_of(core * Q, Q), Q), :]
    gi = half[...] + far[0:Q, :] + own + met[0:Q, :]
    images, texts, w = image_unit[...], text_unit[...], weight[...]
    gi = gi + w * texts.astype(jnp.bfloat16).astype(jnp.float32)
    gi_out[...] = image_inv[...] * (gi - images * jnp.sum(images * gi, axis=-1, keepdims=True))
    gt = gt[...] + w * images.astype(jnp.bfloat16).astype(jnp.float32)
    gt_out[...] = text_inv[...] * (gt - texts * jnp.sum(texts * gt, axis=-1, keepdims=True))
    near = arrived[128:130, 0:128] + met[Q : Q + 2, 0:128]
    near = jnp.where(core == 0, near[:, :Q], near[:, Q:]) + far[Q : Q + 2, 0:Q]
    loss_out[...] = loss[...] + near[0:1] + near[1:2]


def finish(*args):
    width = args[0].shape[1]
    shape = jax.ShapeDtypeStruct((Q, width), jnp.float32)
    return pl.pallas_call(
        finish_kernel,
        out_shape=(
            shape,
            shape,
            jax.ShapeDtypeStruct((1, Q), jnp.float32),
        ),
        compiler_params=pltpu.CompilerParams(vmem_limit_bytes=12 * 1024 * 1024),
        name="finish",
    )(*args)


def tied(*values):
    return lax.optimization_barrier(values)


def gather(a0, t0, core, own):
    r1 = send(a0, split_z=1)
    r4 = send(lax.dynamic_slice_in_dim(a0, core * Q, Q, 0), dz=4)
    xm, xp, c0 = send(t0, dx=1), send(t0, dx=-1), send(t0, fy=3)
    r1, t0, xm, xp, c0 = tied(r1, t0, xm, xp, c0)
    r3, r2 = send(r1, split_z=2), send(r1, split_z=1)
    cm, cp = send(c0, dx=1), send(c0, dx=-1)
    f1, f2 = send(xm[:Q], dx=1), send(xp[Q:], dx=-1)
    r2, r3, r4, cm, cp, f1, f2, *own = tied(r2, r3, r4, cm, cp, f1, f2, *own)
    g1, g2 = send(cm[:Q], dx=1), send(cp[Q:], dx=-1)
    met = send(jnp.concatenate([r1, r2, r3, r4], axis=0), fc=1)
    far = jnp.concatenate([f1, f2], axis=0)
    far_h = jnp.concatenate([g1, g2], axis=0)
    return [a0, r1, r2, r3, r4, met, t0, xm, xp, far, c0, cm, cp, far_h], own


def per_device(image_raw, text_raw, logit_scale_logarithm, logit_offset_bias):
    z, x = lax.axis_index("z"), lax.axis_index("x")
    width = image_raw.shape[1]
    yh, yl, core = lax.axis_index("yh"), lax.axis_index("yl"), lax.axis_index("core")
    f32, f16, bf16 = jnp.float32, jnp.float16, jnp.bfloat16

    def quarter(block, l, c):
        return lax.dynamic_slice_in_dim(block, (l * 2 + c) * Q, Q, 0)

    a0 = normalize(lax.dynamic_slice_in_dim(image_raw, yl * 2 * Q, 2 * Q, 0))[0].astype(bf16)
    t0 = jnp.concatenate([quarter(text_raw, 0, core), quarter(text_raw, 1, core)], axis=0)
    t0 = normalize(t0)[0].astype(bf16)
    image_unit, image_inv = normalize(quarter(image_raw, yl, core))
    text_unit, text_inv = normalize(quarter(text_raw, yl, core))
    temperature, offset = jnp.exp(logit_scale_logarithm[0]), logit_offset_bias[0]
    params = jnp.stack([temperature, offset])

    image_low, text_low = rounded(image_unit), rounded(text_unit)
    match = jnp.sum(image_low * text_low, axis=-1)
    match_logit = temperature * match + offset
    match_loss = jnp.log1p(jnp.exp(-match_logit))
    match_slope = -1.0 / (1.0 + jnp.exp(match_logit))
    match_weight = rounded(temperature * match_slope)
    match_sums = jnp.stack([temperature * jnp.sum(match_slope * match), jnp.sum(match_slope)])
    own = (image_unit, text_unit, image_inv, text_inv, match_loss, match_weight, match_sums)
    chunks, own = gather(a0, t0, core, own)
    image_unit, text_unit, image_inv, text_inv, match_loss, match_weight, match_sums = own
    weights, images, texts, li, lt, sums = pairs_on_device(params, chunks)

    li = li.reshape(-1)
    both = jnp.sum(sums, axis=1) + match_sums
    met = send(jnp.concatenate([li[512:], both]), fc=1)
    met, weights = tied(met, weights)
    li_half, both = li[:512] + met[:512], both + met[512:]
    both = both + send(both, fz=4)
    others = jnp.dot(weights[512:], texts, preferred_element_type=f32).astype(f16)
    loss_rows = [parts_of(li_half[k * 128 - Q : k * 128 + Q]) for k in (1, 2, 3)]
    loss_rows = [extra_rows(parts, width) for parts in (*loss_rows, parts_of(li_half[448:]))]
    both, others, *loss_rows = tied(both, others, *loss_rows)
    both = both + send(both, fz=2)
    rows_met = send(others, fc=1)
    gt16 = lax.dot_general(
        weights, images, (((0,), (0,)), ((), ())), preferred_element_type=f32
    ).astype(f16)
    both, gt16, rows_met = tied(both, gt16, rows_met)
    back_xy = lax.all_to_all(gt16, ("yh", "x", "yl"), 0, 0, tiled=True)
    both = both + send(both, fz=1)
    half = jnp.dot(weights[:512], texts, preferred_element_type=f32) + rows_met.astype(f32)
    flight = half[Q:].astype(f16)
    both, half, flight = tied(both, half, flight)
    far = send(jnp.concatenate([flight[384:], loss_rows[3]]), dz=4)
    three, two, one = (
        send(jnp.concatenate([flight[(k - 1) * 128 : k * 128], loss_rows[k - 1]]), split_z=k) for k in (3, 2, 1)
    )
    plane = jnp.concatenate([lt.reshape(-1), both])
    for move in (dict(fy=1), dict(fx=1), dict(fy=3)):
        plane = plane + send(plane, **move)
    plane, far, three, two, one = tied(plane, far, three, two, one)
    arrived = one.astype(f32) + two.astype(f32) + three.astype(f32)
    theirs = jnp.concatenate([lax.dynamic_slice_in_dim(arrived, (1 - core) * Q, Q, 0), arrived[128:]])
    met = send(theirs, fc=1)
    plane = plane + send(plane, fx=2)
    gt_own = jnp.sum(back_xy.reshape(16, Q, -1).astype(f32), axis=0)
    grad_image, grad_text, image_loss = finish(
        half[:Q], far.astype(f32), arrived, met, gt_own, image_unit, text_unit, image_inv, text_inv,
        match_weight[:, None], (li_half[:Q] + match_loss)[None],
    )
    text_loss = lax.dynamic_slice_in_dim(plane, ((yh * 4 + x) * 2 + yl) * Q, Q, 0) + match_loss
    image_loss, both = image_loss.reshape(Q), plane[1024:]
    return (grad_image, grad_text, image_loss, text_loss, both)


def solution(mesh):
    fine = Mesh(mesh.devices.reshape(YH, NZ, NX, YL, NC), AXES)
    dp = ("yh", "z", "x")
    in_specs = (P(dp, None), P(dp, None), P(), P())
    out_specs = (P(AXES, None), P(AXES, None), P(AXES), P(AXES), P())
    return jax.shard_map(
        per_device, mesh=fine, in_specs=in_specs, out_specs=out_specs, check_vma=False
    )
```
